512 devices in a mesh: dp: 2 (over x_hi), row: 16 (over z), col: 16 (over y, x_lo, core).
Axes of the slice: x: 4 (x_hi: 2, x_lo: 2; x = x_hi * 2 + x_lo), y: 4, z: 16, core: 2. Of those that a mesh axis runs over, the one named last changes fastest.
Arguments:
- gate_query: bfloat16 [2, 16, 512, 2048], P('dp', None, 'row', 'col'), may hold values from -6 to 6
- gate_key: bfloat16 [2, 16, 512, 2048], P('dp', None, 'row', 'col'), may hold values from -6 to 6
- value_input: bfloat16 [2, 16, 512, 2048], P('dp', None, 'row', 'col'), may hold values from -6 to 6
- grad_output: bfloat16 [2, 16, 512, 2048], P('dp', None, 'row', 'col'), may hold values from -6 to 6
- filter_spec: bfloat16 [2, 16, 1024, 2048], P(None, 'row', 'col'), may hold values from -6 to 6
- skip_gain: float32 [16], replicated, may hold values from 0.5 to 2
Outputs:
- grad_query: bfloat16 [2, 16, 512, 2048], P('dp', None, 'row', 'col')
- grad_key: bfloat16 [2, 16, 512, 2048], P('dp', None, 'row', 'col')
- grad_value: bfloat16 [2, 16, 512, 2048], P('dp', None, 'row', 'col')
- filter_grad: bfloat16 [2, 16, 1024, 2048], P(None, 'row', 'col')
The draws below stay inside these ranges and needn't reach their ends.
All inputs are finite; a program needn't handle non-finite values.
Results may differ from the reference program's by a relative error of at most 0.0057.
Values may be sent and summed in bfloat16 or wider, within the bound.
A program may use at most 64 MiB of HBM per device.

```python
import jax
import jax.numpy as jnp
from jax import lax

P_SIZE = 1024
Q = 2048
PH = 512
CH = 16
BATCH = 2


def block_scale(key, dims, cuts, low, top_value):
    def one(axis_at, parts):
        steps = jax.random.uniform(jax.random.fold_in(jax.random.fold_in(key, 6), axis_at), (parts,), jnp.float32, low / len(cuts), top_value / len(cuts))
        return jnp.repeat(jnp.exp(steps), dims[axis_at] // parts).reshape((-1,) + (1,) * (len(dims) - axis_at - 1))

    gain = one(*cuts[0])
    for cut in cuts[1:]:
        gain = gain * one(*cut)
    return gain


def noise(key, shape, scale, reach, shards=(), kind=jnp.bfloat16):
    values = scale * jax.random.normal(key, shape, jnp.float32)
    if shards:
        values = values * block_scale(key, shape, shards, -0.22, 0.18)
    return jnp.clip(values, -reach, reach).astype(kind)


def setup_inputs(seed: int = 0) -> dict:
    key_list = jax.random.split(jax.random.key(seed), 7)
    gate_query = noise(key_list[0], (BATCH, CH, PH, Q), 1.0, 6.0, ((0, 2), (2, 16), (3, 16)))
    gate_key = noise(key_list[1], (BATCH, CH, PH, Q), 1.0, 6.0, ((0, 2), (2, 16), (3, 16)))
    value_input = noise(key_list[2], (BATCH, CH, PH, Q), 1.0, 6.0, ((0, 2), (2, 16), (3, 16)))
    grad_output = noise(key_list[3], (BATCH, CH, PH, Q), 1.0, 6.0, ((0, 2), (2, 16), (3, 16)))
    filter_spec = noise(key_list[4], (2, CH, P_SIZE, Q), 1.0, 6.0, ((1, 16), (2, 16)))
    skip_gain = jnp.clip(jax.random.uniform(key_list[5], (CH,), jnp.float32, 0.5, 2.0), 0.5, 2.0)
    return dict(gate_query=gate_query, gate_key=gate_key, value_input=value_input, grad_output=grad_output, filter_spec=filter_spec, skip_gain=skip_gain)


def channel_terms(mixed_rows, gated_rows, spec_real, spec_imag):
    seq_len = PH * Q
    total_len = P_SIZE * Q
    spectrum = (spec_real + 1j * spec_imag).T.reshape(total_len)

    def one_sequence(running, seq_pair):
        mixed_seq, gated_seq = seq_pair
        mixed_hat = jnp.fft.fft(jnp.pad(mixed_seq.reshape(seq_len), (0, total_len - seq_len)))
        gated_hat = jnp.fft.fft(jnp.pad(gated_seq.reshape(seq_len), (0, total_len - seq_len)))
        conv_seq = jnp.real(jnp.fft.ifft(spectrum * mixed_hat))[:seq_len].reshape(PH, Q)
        corr_seq = jnp.real(jnp.fft.ifft(jnp.conj(spectrum) * gated_hat))[:seq_len].reshape(PH, Q)
        product = jnp.conj(mixed_hat) * gated_hat / total_len
        updated = (running[0] + jnp.real(product), running[1] + jnp.imag(product))
        return updated, (conv_seq, corr_seq)

    zeros = jnp.zeros((total_len,), jnp.float32)
    totals, outputs = lax.scan(one_sequence, (zeros, zeros), (mixed_rows, gated_rows))
    grad_real = totals[0].reshape(Q, P_SIZE).T.astype(jnp.bfloat16)
    grad_imag = totals[1].reshape(Q, P_SIZE).T.astype(jnp.bfloat16)
    return outputs[0], outputs[1], grad_real, grad_imag


def reference(gate_query, gate_key, value_input, grad_output, filter_spec, skip_gain):
    mixed = (gate_key.astype(jnp.float32) * value_input.astype(jnp.float32)).astype(jnp.bfloat16)
    gated = (grad_output.astype(jnp.float32) * gate_query.astype(jnp.float32)).astype(jnp.bfloat16)
    mixed_wide = lax.optimization_barrier(mixed).astype(jnp.float32)
    gated_wide = lax.optimization_barrier(gated).astype(jnp.float32)
    spec_wide = filter_spec.astype(jnp.float32)

    def per_channel(channel):
        return channel_terms(mixed_wide[:, channel], gated_wide[:, channel], spec_wide[0, channel], spec_wide[1, channel])

    convolved, correlated, grad_real, grad_imag = lax.map(per_channel, jnp.arange(CH, dtype=jnp.int32))
    convolved = jnp.swapaxes(convolved, 0, 1)
    correlated = jnp.swapaxes(correlated, 0, 1)
    gain_wide = skip_gain[None, :, None, None]
    grad_query = (grad_output.astype(jnp.float32) * (convolved + gain_wide * mixed_wide)).astype(jnp.bfloat16)
    grad_mixed = correlated + gain_wide * gated_wide
    grad_key = (grad_mixed * value_input.astype(jnp.float32)).astype(jnp.bfloat16)
    grad_value = (grad_mixed * gate_key.astype(jnp.float32)).astype(jnp.bfloat16)
    filter_grad = jnp.stack([grad_real, grad_imag])
    return grad_query, grad_key, grad_value, filter_grad
```

```python
import functools
import math

import jax
import jax.numpy as jnp
import numpy as np
from jax import lax
from jax.experimental import pallas as pl
from jax.experimental.pallas import tpu as pltpu
from jax.sharding import PartitionSpec as P

MESH = pl.DeviceIdType.MESH
BF16 = jnp.bfloat16
F32 = jnp.float32


def split_table(table):
    high = table.astype(np.float32).astype(BF16)
    low = (table - high.astype(np.float64)).astype(np.float32).astype(BF16)
    return high, low


def make_tables(rows_total, cols_total, col_devices):
    half = rows_total // 2
    span = cols_total // col_devices
    keep = rows_total // col_devices
    total = rows_total * cols_total
    freq = np.arange(rows_total).reshape(col_devices, 1, keep, 1)
    angle = 2 * np.pi / rows_total * (freq * np.arange(half) % rows_total)
    row_table = np.concatenate([np.cos(angle), -np.sin(angle)], axis=1)
    row_table = row_table.reshape(col_devices, 2 * keep, half)
    forward_high, forward_low = split_table(row_table)
    inverse_rows = (row_table.reshape(rows_total * 2, half).T / total).astype(np.float32).astype(BF16)
    angle = 2 * np.pi / total * (np.arange(rows_total)[:, None] * np.arange(span) % total)
    twist = np.stack([np.cos(angle), -np.sin(angle)]).astype(np.float32)
    lanes = np.arange(128)
    angle = 2 * np.pi / total * (np.arange(rows_total)[:, None] * lanes * span % total)
    place = np.stack([np.cos(angle), -np.sin(angle)]).astype(np.float32)
    angle = 2 * np.pi / cols_total * (np.arange(col_devices)[:, None] * np.arange(span) % cols_total)
    inner = np.stack([np.cos(angle), -np.sin(angle)]).astype(np.float32)
    angle = 2 * np.pi / span * (np.arange(span)[:, None] * np.arange(span) % span)
    cosine, sine = np.cos(angle), np.sin(angle)
    lane_high, lane_low = split_table(np.block([[cosine, -sine], [sine, cosine]]))
    lane_inverse = np.block([[cosine, sine], [-sine, cosine]]).astype(np.float32).astype(BF16)
    order = np.arange(cols_total).reshape(span, col_devices).T.reshape(-1)
    shuffle = np.zeros((cols_total, cols_total), np.float32)
    shuffle[order, np.arange(cols_total)] = 1
    return dict(
        forward_high=forward_high,
        forward_low=forward_low,
        inverse_rows=inverse_rows,
        twist=twist,
        place=place,
        inner=inner,
        lane_high=lane_high,
        lane_low=lane_low,
        lane_inverse=lane_inverse,
        shuffle=shuffle.astype(BF16),
        unshuffle=shuffle.T.astype(BF16),
    )


def times(a, b, cos_part, sin_part):
    return a * cos_part - b * sin_part, a * sin_part + b * cos_part


def small_fft(values, sign):
    n = len(values)
    if n == 1:
        return values
    if n == 2:
        (a, b), (c, d) = values
        return [(a + c, b + d), (a - c, b - d)]
    if n == 4:
        (a, b), (c, d), (e, f), (g, h) = values
        s0r, s0i, d0r, d0i = a + e, b + f, a - e, b - f
        s1r, s1i, d1r, d1i = c + g, d + h, c - g, d - h
        tr, ti = (-d1i, d1r) if sign > 0 else (d1i, -d1r)
        return [
            (s0r + s1r, s0i + s1i),
            (d0r + tr, d0i + ti),
            (s0r - s1r, s0i - s1i),
            (d0r - tr, d0i - ti),
        ]
    radix = 4 if n % 4 == 0 else 2
    other = n // radix
    out = [None] * n
    parts = []
    for b in range(radix):
        part = small_fft(values[b::radix], sign)
        turned = []
        for k, (re, im) in enumerate(part):
            turn = (b * k) % n
            if turn == 0:
                turned.append((re, im))
            elif 4 * turn == n:
                turned.append((-im, re) if sign > 0 else (im, -re))
            elif 8 * turn == n or 8 * turn == 3 * n:
                w = math.sqrt(0.5)
                c = w if 8 * turn == n else -w
                s = sign * w
                turned.append(times(re, im, c, s))
            else:
                angle = sign * 2 * math.pi * turn / n
                turned.append(times(re, im, math.cos(angle), math.sin(angle)))
        parts.append(turned)
    for k in range(other):
        column = small_fft([parts[b][k] for b in range(radix)], sign)
        for m in range(radix):
            out[k + other * m] = column[m]
    return out


def ring_order(size):
    return sorted(range(1, size), key=lambda s: -min(s, size - s))


def kernel(
    dims,
    gq, gk, vi, go, spec, gain,
    fwd_high_hbm, fwd_low_hbm, inv_hbm, twist_hbm, place_hbm, inner, lane_high, lane_low, lane_inv,
    shuffle_hbm, unshuffle_hbm,
    grad_query, grad_key, grad_value, filter_grad,
    fwd_high, fwd_low, inv_rows, twist, place, shuffle, unshuffle,
    prod, recv1, send2, recv2, send3, recv3, send4, recv4,
    stage, wide, spectra, sint, turned, fsend, frecv,
    load_sem, own_sem, s1, r1, s2, r2, s3, r3, s4, r4, sf, rf,
):
    row_devices, col_devices, keep, span, rows_here = dims
    me_row = lax.axis_index("row")
    me_col = lax.axis_index("col")
    me_dp = lax.axis_index("dp")
    other_dp = 1 - me_dp
    block = 2 * keep
    rows_total = col_devices * keep
    half = rows_total // 2

    barrier = pltpu.get_barrier_semaphore()
    for s in range(1, row_devices):
        pl.semaphore_signal(
            barrier, inc=1, device_id={"row": lax.rem(me_row + s, row_devices)}, device_id_type=MESH
        )
    for s in range(1, col_devices):
        pl.semaphore_signal(
            barrier, inc=1, device_id={"col": lax.rem(me_col + s, col_devices)}, device_id_type=MESH
        )
    pl.semaphore_signal(barrier, inc=1, device_id={"dp": other_dp}, device_id_type=MESH)

    loads = [
        (shuffle_hbm, shuffle),
        (fwd_high_hbm, fwd_high),
        (fwd_low_hbm, fwd_low),
        (twist_hbm, twist),
        (place_hbm, place),
        (inv_hbm, inv_rows),
        (unshuffle_hbm, unshuffle),
    ]
    loads = [
        pltpu.make_async_copy(src, dst, load_sem.at[i]) for i, (src, dst) in enumerate(loads)
    ]
    for copy in loads:
        copy.start()

    prod[0] = (gk[...].astype(F32) * vi[...].astype(F32)).astype(BF16)
    prod[1] = (go[...].astype(F32) * gq[...].astype(F32)).astype(BF16)
    pl.semaphore_wait(barrier, row_devices + col_devices - 1)

    def exchange(axis, me, size, a, send, recv, send_sem, recv_sem, index):
        return pltpu.make_async_remote_copy(
            src_ref=send.at[a, index],
            dst_ref=recv.at[a, me],
            send_sem=send_sem.at[a, index],
            recv_sem=recv_sem.at[a, me],
            device_id={axis: index},
            device_id_type=MESH,
        )

    def own(me, a, send, recv, step):
        return pltpu.make_async_copy(send.at[a, me], recv.at[a, me], own_sem.at[step, a])

    def wait_recv(axis, me, size, a, send, recv, send_sem, recv_sem, step):
        def body(s, carry):
            source = lax.rem(me + s, size)
            pltpu.make_async_remote_copy(
                src_ref=send.at[a, source],
                dst_ref=recv.at[a, source],
                send_sem=send_sem.at[a, source],
                recv_sem=recv_sem.at[a, source],
                device_id={axis: source},
                device_id_type=MESH,
            ).wait_recv()
            return carry

        lax.fori_loop(1, size, body, 0)
        own(me, a, send, recv, step).wait()

    def wait_send(axis, me, size, a, send, recv, send_sem, recv_sem):
        def body(s, carry):
            exchange(axis, me, size, a, send, recv, send_sem, recv_sem, lax.rem(me + s, size)).wait_send()
            return carry

        lax.fori_loop(1, size, body, 0)

    row = ("row", me_row, row_devices)
    col = ("col", me_col, col_devices)

    for a in range(2):
        for s in ring_order(row_devices):
            exchange(*row, a, prod, recv1, s1, r1, lax.rem(me_row + s, row_devices)).start()
        own(me_row, a, prod, recv1, 0).start()

    loads[0].wait()
    planes = spec.shape[0] * spec.shape[1]
    internal = jnp.dot(
        spec[...].reshape(planes, spec.shape[2]), shuffle[...], preferred_element_type=F32
    )
    for k in range(col_devices):
        sint[0, k] = internal[:keep, k * span : (k + 1) * span]
        sint[1, k] = internal[keep:, k * span : (k + 1) * span]

    for i in range(1, 6):
        loads[i].wait()
    for c in range(col_devices):
        rows = pl.ds(c * keep, keep)
        lane = lax.broadcasted_iota(jnp.int32, (keep, 128), 1) == me_col
        pr = jnp.sum(jnp.where(lane, place[0, rows], 0.0), axis=1, keepdims=True)
        pi = jnp.sum(jnp.where(lane, place[1, rows], 0.0), axis=1, keepdims=True)
        tr, ti = times(twist[0, rows], twist[1, rows], pr, pi)
        turned[0, c] = tr
        turned[1, c] = ti

    def row_stage(a):
        wait_recv(*row, a, prod, recv1, s1, r1, 0)
        tokens = recv1[a].reshape(half, span)

        def body(s, carry):
            d = lax.rem(me_col + 1 + s, col_devices)
            z = jnp.dot(fwd_high[d], tokens, preferred_element_type=F32)
            z = z + jnp.dot(fwd_low[d], tokens, preferred_element_type=F32)
            re, im = times(z[:keep], z[keep:], turned[0, d], turned[1, d])
            send2[a, d] = jnp.concatenate([re, im], axis=0).astype(BF16)

            @pl.when(s < col_devices - 1)
            def _():
                exchange(*col, a, send2, recv2, s2, r2, d).start()

            return carry

        lax.fori_loop(0, col_devices, body, 0)
        own(me_col, a, send2, recv2, 1).start()

    def col_stage(a):
        wait_recv(*col, a, send2, recv2, s2, r2, 1)

        def widen(c, carry):
            stage[c] = recv2[a, c].astype(F32)
            return carry

        lax.fori_loop(0, col_devices, widen, 0)

        def forward(t, carry):
            re_rows = pl.ds(pl.multiple_of(t * 8, 8), 8)
            im_rows = pl.ds(pl.multiple_of(keep + t * 8, 8), 8)
            values = [(stage[c, re_rows], stage[c, im_rows]) for c in range(col_devices)]
            values = small_fft(values, -1)
            for k, (re, im) in enumerate(values):
                if k:
                    re, im = times(re, im, inner[0, k : k + 1], inner[1, k : k + 1])
                wide[k, re_rows, :span] = re
                wide[k, re_rows, span:] = im
            return carry

        lax.fori_loop(0, keep // 8, forward, 0)

        def middle(k, carry):
            y = wide[k].astype(BF16)
            x = jnp.dot(y, lane_high[...], preferred_element_type=F32)
            x = x + jnp.dot(y, lane_low[...], preferred_element_type=F32)
            spectra[a, k] = x
            sr, si = sint[0, k], sint[1, k]
            if a == 1:
                si = -si
            re, im = times(x[:, :span], x[:, span:], sr, si)
            v = jnp.concatenate([re, im], axis=1).astype(BF16)
            w = jnp.dot(v, lane_inv[...], preferred_element_type=F32)
            re, im = times(w[:, :span], w[:, span:], inner[0, pl.ds(k, 1)], -inner[1, pl.ds(k, 1)])
            wide[k, :, :span] = re
            wide[k, :, span:] = im
            return carry

        lax.fori_loop(0, col_devices, middle, 0)

        def backward(t, carry):
            re_rows = pl.ds(pl.multiple_of(t * 8, 8), 8)
            im_rows = pl.ds(pl.multiple_of(keep + t * 8, 8), 8)
            values = [(wide[k, re_rows, :span], wide[k, re_rows, span:]) for k in range(col_devices)]
            values = small_fft(values, 1)
            for c, (re, im) in enumerate(values):
                stage[c, re_rows] = re
                stage[c, im_rows] = im
            return carry

        lax.fori_loop(0, keep // 8, backward, 0)

        def narrow(s, carry):
            d = lax.rem(me_col + 1 + s, col_devices)
            send3[a, d] = stage[d].astype(BF16)

            @pl.when(s < col_devices - 1)
            def _():
                exchange(*col, a, send3, recv3, s3, r3, d).start()

            return carry

        lax.fori_loop(0, col_devices, narrow, 0)
        own(me_col, a, send3, recv3, 2).start()

    def back_stage(a):
        wait_recv(*col, a, send3, recv3, s3, r3, 2)
        total = None
        group = max(1, col_devices // 4)
        for g in range(0, col_devices, group):
            parts = []
            for c in range(g, g + group):
                got = recv3[a, c].astype(F32)
                re, im = times(got[:keep], got[keep:], turned[0, c], -turned[1, c])
                parts += [re, im]
            w = jnp.concatenate(parts, axis=0).astype(BF16)
            term = jnp.dot(
                inv_rows[:, g * block : (g + group) * block], w, preferred_element_type=F32
            )
            total = term if total is None else total + term
        send4[a] = total.astype(BF16).reshape(row_devices, rows_here, span)
        for s in ring_order(row_devices):
            exchange(*row, a, send4, recv4, s4, r4, lax.rem(me_row + s, row_devices)).start()
        own(me_row, a, send4, recv4, 3).start()

    row_stage(0)
    row_stage(1)
    col_stage(0)
    col_stage(1)

    scale = 1.0 / (rows_total * col_devices * span)
    for k in range(col_devices):
        m, g = spectra[0, k], spectra[1, k]
        mr, mi, gr, gi = m[:, :span], m[:, span:], g[:, :span], g[:, span:]
        both = jnp.concatenate([mr * gr + mi * gi, mr * gi - mi * gr], axis=0) * scale
        fsend[:, k * span : (k + 1) * span] = both.astype(BF16)
    fcopy = pltpu.make_async_remote_copy(
        src_ref=fsend,
        dst_ref=frecv,
        send_sem=sf,
        recv_sem=rf,
        device_id={"dp": other_dp},
        device_id_type=MESH,
    )
    fcopy.start()

    back_stage(0)
    back_stage(1)

    fcopy.wait_recv()
    loads[6].wait()
    fsum = (fsend[...].astype(F32) + frecv[...].astype(F32)).astype(BF16)
    natural = jnp.dot(fsum, unshuffle[...], preferred_element_type=F32).astype(BF16)
    filter_grad[...] = natural.reshape(filter_grad.shape)

    wait_recv(*row, 0, send4, recv4, s4, r4, 3)
    for c in range(row_devices):
        wide_gain = gain[c]
        conv = recv4[0, c].astype(F32) + wide_gain * prod[0, c].astype(F32)
        grad_query[c] = (go[c].astype(F32) * conv).astype(BF16)
    wait_recv(*row, 1, send4, recv4, s4, r4, 3)
    for c in range(row_devices):
        wide_gain = gain[c]
        mixed_grad = recv4[1, c].astype(F32) + wide_gain * prod[1, c].astype(F32)
        grad_key[c] = (mixed_grad * vi[c].astype(F32)).astype(BF16)
        grad_value[c] = (mixed_grad * gk[c].astype(F32)).astype(BF16)

    for a in range(2):
        wait_send(*row, a, prod, recv1, s1, r1)
        wait_send(*col, a, send2, recv2, s2, r2)
        wait_send(*col, a, send3, recv3, s3, r3)
        wait_send(*row, a, send4, recv4, s4, r4)
    fcopy.wait_send()


def shards(tables, row_devices, col_devices, gate_query, gate_key, value_input, grad_output, filter_spec, skip_gain):
    _, channels, rows_here, span = gate_query.shape
    keep = filter_spec.shape[2]
    cols_total = filter_spec.shape[3]
    rows_total = keep * col_devices
    half = rows_total // 2
    block = 2 * keep
    dims = (row_devices, col_devices, keep, span, rows_here)
    vmem = pl.BlockSpec(memory_space=pltpu.VMEM)
    anywhere = pl.BlockSpec(memory_space=pl.ANY)
    token = jax.ShapeDtypeStruct((channels, rows_here, span), BF16)
    names = [
        "forward_high", "forward_low", "inverse_rows", "twist", "place",
        "inner", "lane_high", "lane_low", "lane_inverse", "shuffle", "unshuffle",
    ]
    small = {"inner", "lane_high", "lane_low", "lane_inverse"}
    dma = pltpu.SemaphoreType.DMA
    tok = (2, row_devices, rows_here, span)
    mid = (2, col_devices, block, span)
    outs = pl.pallas_call(
        functools.partial(kernel, dims),
        out_shape=[token, token, token, jax.ShapeDtypeStruct((2, keep, cols_total), BF16)],
        in_specs=[vmem] * 5
        + [pl.BlockSpec(memory_space=pltpu.SMEM)]
        + [vmem if name in small else anywhere for name in names],
        out_specs=[vmem] * 4,
        scratch_shapes=[
            pltpu.VMEM((col_devices, block, half), BF16),
            pltpu.VMEM((col_devices, block, half), BF16),
            pltpu.VMEM((half, col_devices * block), BF16),
            pltpu.VMEM((2, rows_total, span), F32),
            pltpu.VMEM((2, rows_total, 128), F32),
            pltpu.VMEM((cols_total, cols_total), BF16),
            pltpu.VMEM((cols_total, cols_total), BF16),
            pltpu.VMEM(tok, BF16),
            pltpu.VMEM(tok, BF16),
            pltpu.VMEM(mid, BF16),
            pltpu.VMEM(mid, BF16),
            pltpu.VMEM(mid, BF16),
            pltpu.VMEM(mid, BF16),
            pltpu.VMEM(tok, BF16),
            pltpu.VMEM(tok, BF16),
            pltpu.VMEM((col_devices, block, span), F32),
            pltpu.VMEM((col_devices, keep, 2 * span), F32),
            pltpu.VMEM((2, col_devices, keep, 2 * span), F32),
            pltpu.VMEM((2, col_devices, keep, span), F32),
            pltpu.VMEM((2, col_devices, keep, span), F32),
            pltpu.VMEM((block, cols_total), BF16),
            pltpu.VMEM((block, cols_total), BF16),
            dma((7,)),
            dma((4, 2)),
            dma((2, row_devices)), dma((2, row_devices)),
            dma((2, col_devices)), dma((2, col_devices)),
            dma((2, col_devices)), dma((2, col_devices)),
            dma((2, row_devices)), dma((2, row_devices)),
            dma, dma,
        ],
        compiler_params=pltpu.CompilerParams(
            collective_id=0, has_side_effects=True, vmem_limit_bytes=56 * 1024 * 1024
        ),
        name="hyena_backward",
    )(
        gate_query[0], gate_key[0], value_input[0], grad_output[0], filter_spec[:, 0], skip_gain,
        *[jnp.asarray(tables[name]) for name in names],
    )
    return (outs[0][None], outs[1][None], outs[2][None], outs[3][:, None])


def solution(mesh):
    row_devices, col_devices = mesh.shape["row"], mesh.shape["col"]
    tokens = P("dp", None, "row", "col")
    freq = P(None, "row", "col", None)

    def run(gate_query, gate_key, value_input, grad_output, filter_spec, skip_gain):
        tables = make_tables(filter_spec.shape[2], filter_spec.shape[3], col_devices)
        return jax.shard_map(
            functools.partial(shards, tables, row_devices, col_devices),
            mesh=mesh,
            in_specs=(tokens, tokens, tokens, tokens, freq, P()),
            out_specs=(tokens, tokens, tokens, freq),
            check_vma=False,
        )(gate_query, gate_key, value_input, grad_output, filter_spec, skip_gain)

    return run
```

```python
import functools
import math

import jax
import jax.numpy as jnp
import numpy as np
from jax import lax
from jax.experimental import pallas as pl
from jax.experimental.pallas import tpu as pltpu
from jax.sharding import PartitionSpec as P

MESH = pl.DeviceIdType.MESH
BF16 = jnp.bfloat16
F32 = jnp.float32


def split_table(table):
    high = table.astype(np.float32).astype(BF16)
    low = (table - high.astype(np.float64)).astype(np.float32).astype(BF16)
    return high, low


def make_tables(rows_total, cols_total, col_devices):
    half = rows_total // 2
    span = cols_total // col_devices
    keep = rows_total // col_devices
    total = rows_total * cols_total
    act = keep // 2 + 8
    freq = keep * np.arange(col_devices)[:, None] + np.arange(act)
    angle = 2 * np.pi / rows_total * (freq[:, None, :, None] * np.arange(half) % rows_total)
    row_table = np.concatenate([np.cos(angle), -np.sin(angle)], axis=1)
    row_table[:, :, keep // 2 + 1 :] = 0
    row_table = row_table.reshape(col_devices * 2 * act, half)
    group = math.gcd(col_devices, 4)
    forward_high, forward_low = split_table(row_table.reshape(-1, group * 2 * act, half))
    inverse_rows = (row_table.T / total).astype(np.float32).astype(BF16)
    freq = freq.reshape(-1, 1)
    flip_lanes = np.eye(span)[::-1].astype(np.float32).astype(BF16)
    flip_rows = np.zeros((2, act, 2, keep // 2), np.float32)
    for r in range(1, keep // 2):
        flip_rows[0, r, 0, keep // 2 - r] = 1
        flip_rows[1, r, 1, keep // 2 - r] = -1
    flip_rows = flip_rows.reshape(2 * act, keep).astype(BF16)
    angle = 2 * np.pi / total * (freq * np.arange(span) % total)
    twist = np.stack([np.cos(angle), -np.sin(angle)]).astype(np.float32)
    lanes = np.arange(128)
    angle = 2 * np.pi / total * (freq * lanes * span % total)
    place = np.stack([np.cos(angle), -np.sin(angle)]).astype(np.float32)
    angle = 2 * np.pi / cols_total * (np.arange(col_devices)[:, None] * np.arange(span) % cols_total)
    inner = np.stack([np.cos(angle), -np.sin(angle)]).astype(np.float32)
    angle = 2 * np.pi / span * (np.arange(span)[:, None] * np.arange(span) % span)
    cosine, sine = np.cos(angle), np.sin(angle)
    lane_high, lane_low = split_table(np.block([[cosine, -sine], [sine, cosine]]))
    lane_inverse = np.block([[cosine, sine], [-sine, cosine]]).astype(np.float32).astype(BF16)
    return dict(
        forward_high=forward_high,
        forward_low=forward_low,
        inverse_rows=inverse_rows,
        twist=twist,
        place=place,
        inner=inner,
        lane_high=lane_high,
        lane_low=lane_low,
        lane_inverse=lane_inverse,
        flip_lanes=flip_lanes,
        flip_rows=flip_rows,
        unflip_rows=flip_rows.T,
    )


def times(a, b, cos_part, sin_part):
    return a * cos_part - b * sin_part, a * sin_part + b * cos_part


def small_fft(values, sign):
    n = len(values)
    if n == 1:
        return values
    if n == 2:
        (a, b), (c, d) = values
        return [(a + c, b + d), (a - c, b - d)]
    if n == 4:
        (a, b), (c, d), (e, f), (g, h) = values
        s0r, s0i, d0r, d0i = a + e, b + f, a - e, b - f
        s1r, s1i, d1r, d1i = c + g, d + h, c - g, d - h
        tr, ti = (-d1i, d1r) if sign > 0 else (d1i, -d1r)
        return [
            (s0r + s1r, s0i + s1i),
            (d0r + tr, d0i + ti),
            (s0r - s1r, s0i - s1i),
            (d0r - tr, d0i - ti),
        ]
    radix = 4 if n % 4 == 0 else 2
    other = n // radix
    out = [None] * n
    parts = []
    for b in range(radix):
        part = small_fft(values[b::radix], sign)
        turned = []
        for k, (re, im) in enumerate(part):
            turn = (b * k) % n
            if turn == 0:
                turned.append((re, im))
            elif 4 * turn == n:
                turned.append((-im, re) if sign > 0 else (im, -re))
            elif 8 * turn == n or 8 * turn == 3 * n:
                w = math.sqrt(0.5)
                c = w if 8 * turn == n else -w
                s = sign * w
                turned.append(times(re, im, c, s))
            else:
                angle = sign * 2 * math.pi * turn / n
                turned.append(times(re, im, math.cos(angle), math.sin(angle)))
        parts.append(turned)
    for k in range(other):
        column = small_fft([parts[b][k] for b in range(radix)], sign)
        for m in range(radix):
            out[k + other * m] = column[m]
    return out


def ring_order(size):
    return sorted(range(1, size), key=lambda s: -min(s, size - s))


def kernel(
    dims,
    gq_hbm, gk_hbm, vi_hbm, go_hbm, spec_hbm, gain,
    fwd_high_hbm, fwd_low_hbm, inv_hbm, twist_hbm, place_hbm, inner_hbm, lane_high_hbm, lane_low_hbm,
    lane_inv_hbm, flip_lanes_hbm, flip_rows_hbm, unflip_rows_hbm,
    grad_query_hbm, grad_key_hbm, grad_value_hbm, filter_grad_hbm,
    gq, gk, vi, go, spec,
    fwd_high, fwd_low, inv_rows, twist, place, inner, lane_high, lane_low,
    lane_inv, flip_lanes, flip_rows, unflip_rows,
    grad_query, grad_key, grad_value, filter_grad, flip,
    prod, recv1, send2, recv2, send3, recv3, send4, recv4,
    stage, wide, spectra, smir, sint, turned, fsend, frecv, fown, fmsend, fmrecv,
    load_sem, out_sem, own_sem, s1, r1, s2, r2, s3, r3, s4, r4, sf, rf, sfm, rfm, sm, rm,
):
    row_devices, col_devices, keep, span, rows_here = dims
    me_row = lax.axis_index("row")
    me_col = lax.axis_index("col")
    me_dp = lax.axis_index("dp")
    other_dp = 1 - me_dp
    act = keep // 2 + 8
    block = 2 * act
    rows_total = col_devices * keep
    half = rows_total // 2

    barrier = pltpu.get_barrier_semaphore()
    for s in range(1, row_devices):
        pl.semaphore_signal(
            barrier, inc=1, device_id={"row": lax.rem(me_row + s, row_devices)}, device_id_type=MESH
        )
    for s in range(1, col_devices):
        pl.semaphore_signal(
            barrier, inc=1, device_id={"col": lax.rem(me_col + s, col_devices)}, device_id_type=MESH
        )
    pl.semaphore_signal(barrier, inc=1, device_id={"dp": other_dp}, device_id_type=MESH)

    loads = [
        (gk_hbm, gk), (vi_hbm, vi), (go_hbm, go), (gq_hbm, gq), (spec_hbm, spec),
        (twist_hbm, twist), (place_hbm, place),
        (fwd_high_hbm, fwd_high), (fwd_low_hbm, fwd_low),
        (flip_lanes_hbm, flip_lanes), (flip_rows_hbm, flip_rows), (unflip_rows_hbm, unflip_rows),
        (inner_hbm, inner), (lane_high_hbm, lane_high), (lane_low_hbm, lane_low), (lane_inv_hbm, lane_inv),
        (inv_hbm, inv_rows),
    ]
    loads = [
        pltpu.make_async_copy(src, dst, load_sem.at[i]) for i, (src, dst) in enumerate(loads)
    ]
    for copy in loads:
        copy.start()

    def exchange(axis, me, size, a, send, recv, send_sem, recv_sem, index):
        return pltpu.make_async_remote_copy(
            src_ref=send.at[a, index],
            dst_ref=recv.at[a, me],
            send_sem=send_sem.at[a, index],
            recv_sem=recv_sem.at[a, me],
            device_id={axis: index},
            device_id_type=MESH,
        )

    def own(me, a, send, recv, step):
        return pltpu.make_async_copy(send.at[a, me], recv.at[a, me], own_sem.at[step, a])

    def wait_recv(axis, me, size, a, send, recv, send_sem, recv_sem, step):
        def body(s, carry):
            source = lax.rem(me + s, size)
            pltpu.make_async_remote_copy(
                src_ref=send.at[a, source],
                dst_ref=recv.at[a, source],
                send_sem=send_sem.at[a, source],
                recv_sem=recv_sem.at[a, source],
                device_id={axis: source},
                device_id_type=MESH,
            ).wait_recv()
            return carry

        lax.fori_loop(1, size, body, 0)
        own(me, a, send, recv, step).wait()

    def wait_send(axis, me, size, a, send, recv, send_sem, recv_sem):
        def body(s, carry):
            exchange(axis, me, size, a, send, recv, send_sem, recv_sem, lax.rem(me + s, size)).wait_send()
            return carry

        lax.fori_loop(1, size, body, 0)

    row = ("row", me_row, row_devices)
    col = ("col", me_col, col_devices)

    for a, (left, right) in enumerate([(gk, vi), (go, gq)]):
        loads[2 * a].wait()
        loads[2 * a + 1].wait()
        prod[a] = (left[...].astype(F32) * right[...].astype(F32)).astype(BF16)
        if a == 0:
            pl.semaphore_wait(barrier, row_devices + col_devices - 1)
        for s in ring_order(row_devices):
            exchange(*row, a, prod, recv1, s1, r1, lax.rem(me_row + s, row_devices)).start()
        own(me_row, a, prod, recv1, 0).start()

    loads[4].wait()
    partner = {"col": col_devices - 1 - me_col}
    mirror = pltpu.make_async_remote_copy(
        src_ref=spec.at[:, pl.ds(keep // 2, keep // 2)],
        dst_ref=smir,
        send_sem=sm,
        recv_sem=rm,
        device_id=partner,
        device_id_type=MESH,
    )
    mirror.start()

    loads[5].wait()
    loads[6].wait()
    for c in range(col_devices):
        rows = pl.ds(c * act, act)
        lane = lax.broadcasted_iota(jnp.int32, (act, 128), 1) == me_col
        pr = jnp.sum(jnp.where(lane, place[0, rows], 0.0), axis=1, keepdims=True)
        pi = jnp.sum(jnp.where(lane, place[1, rows], 0.0), axis=1, keepdims=True)
        tr, ti = times(twist[0, rows], twist[1, rows], pr, pi)
        turned[0, c] = tr
        turned[1, c] = ti

    def spectrum_stage():
        mirror.wait_recv()
        loads[9].wait()
        loads[10].wait()
        for t in range(col_devices):
            lanes = slice(t * span, (t + 1) * span)
            far = slice((col_devices - 1 - t) * span, (col_devices - t) * span)
            got = smir[:, :, far].reshape(keep, span)
            got = jnp.dot(got, flip_lanes[...], preferred_element_type=F32).astype(BF16)
            got = jnp.dot(flip_rows[...], got, preferred_element_type=F32)
            tile = spec[:, :, lanes].astype(F32)[:, :act].reshape(block, span)
            flip[lanes, :block] = (tile + got).T
        for k in range(col_devices):
            tile = flip[pl.ds(k, span, stride=col_devices), :block].T
            sint[0, k] = tile[:act]
            sint[1, k] = tile[act:]

    def row_stage(a):
        wait_recv(*row, a, prod, recv1, s1, r1, 0)
        tokens = recv1[a].reshape(half, span)

        groups = fwd_high.shape[0]
        group = col_devices // groups

        def body(s, carry):
            g = lax.rem(lax.div(me_col, group) + 1 + s, groups)
            z = jnp.dot(fwd_high[g], tokens, preferred_element_type=F32)
            z = z + jnp.dot(fwd_low[g], tokens, preferred_element_type=F32)
            for i in range(group):
                d = g * group + i
                zr = z[i * block : i * block + act]
                zi = z[i * block + act : (i + 1) * block]
                re, im = times(zr, zi, turned[0, d], turned[1, d])
                send2[a, d] = jnp.concatenate([re, im], axis=0).astype(BF16)

                @pl.when(d != me_col)
                def _():
                    exchange(*col, a, send2, recv2, s2, r2, d).start()

            return carry

        lax.fori_loop(0, groups, body, 0)
        own(me_col, a, send2, recv2, 1).start()

    def col_stage(a):
        wait_recv(*col, a, send2, recv2, s2, r2, 1)

        def widen(c, carry):
            stage[c] = recv2[a, c].astype(F32)
            return carry

        lax.fori_loop(0, col_devices, widen, 0)

        def forward(t, carry):
            re_rows = pl.ds(pl.multiple_of(t * 8, 8), 8)
            im_rows = pl.ds(pl.multiple_of(act + t * 8, 8), 8)
            values = [(stage[c, re_rows], stage[c, im_rows]) for c in range(col_devices)]
            values = small_fft(values, -1)
            for k, (re, im) in enumerate(values):
                if k:
                    re, im = times(re, im, inner[0, k : k + 1], inner[1, k : k + 1])
                wide[k, re_rows, :span] = re
                wide[k, re_rows, span:] = im
            return carry

        lax.fori_loop(0, act // 8, forward, 0)

        group = math.gcd(col_devices, 8)

        def middle(g, carry):
            some = pl.ds(g * group, group)
            y = wide[some].reshape(group * act, 2 * span).astype(BF16)
            x = jnp.dot(y, lane_high[...], preferred_element_type=F32)
            x = x + jnp.dot(y, lane_low[...], preferred_element_type=F32)
            spectra[a, some] = x.reshape(group, act, 2 * span)
            sr = sint[0, some].reshape(group * act, span)
            si = sint[1, some].reshape(group * act, span)
            if a == 1:
                si = -si
            re, im = times(x[:, :span], x[:, span:], sr, si)
            v = jnp.concatenate([re, im], axis=1).astype(BF16)
            w = jnp.dot(v, lane_inv[...], preferred_element_type=F32)
            w = w.reshape(group, act, 2 * span)
            ir, ii = inner[0, some], inner[1, some]
            re, im = times(w[:, :, :span], w[:, :, span:], ir[:, None], -ii[:, None])
            wide[some, :, :span] = re
            wide[some, :, span:] = im
            return carry

        lax.fori_loop(0, col_devices // group, middle, 0)

        def backward(t, carry):
            re_rows = pl.ds(pl.multiple_of(t * 8, 8), 8)
            im_rows = pl.ds(pl.multiple_of(act + t * 8, 8), 8)
            values = [(wide[k, re_rows, :span], wide[k, re_rows, span:]) for k in range(col_devices)]
            values = small_fft(values, 1)
            for c, (re, im) in enumerate(values):
                stage[c, re_rows] = re
                stage[c, im_rows] = im
            return carry

        lax.fori_loop(0, act // 8, backward, 0)

        def narrow(s, carry):
            d = lax.rem(me_col + 1 + s, col_devices)
            send3[a, d] = stage[d].astype(BF16)

            @pl.when(s < col_devices - 1)
            def _():
                exchange(*col, a, send3, recv3, s3, r3, d).start()

            return carry

        lax.fori_loop(0, col_devices, narrow, 0)
        own(me_col, a, send3, recv3, 2).start()

    def back_stage(a):
        wait_recv(*col, a, send3, recv3, s3, r3, 2)
        parts = []
        for c in range(col_devices):
            got = recv3[a, c].astype(F32)
            re, im = times(got[:act], got[act:], turned[0, c], -turned[1, c])
            parts += [re, im]
        w = jnp.concatenate(parts, axis=0).astype(BF16)
        total = jnp.dot(inv_rows[...], w, preferred_element_type=F32)
        send4[a] = total.astype(BF16).reshape(row_devices, rows_here, span)
        for s in ring_order(row_devices):
            exchange(*row, a, send4, recv4, s4, r4, lax.rem(me_row + s, row_devices)).start()
        own(me_row, a, send4, recv4, 3).start()

    loads[7].wait()
    loads[8].wait()
    row_stage(0)
    spectrum_stage()
    row_stage(1)
    for i in range(12, 16):
        loads[i].wait()
    col_stage(0)
    col_stage(1)

    scale = 1.0 / (rows_total * col_devices * span)
    chunk = math.gcd(col_devices, 4)
    fcopies = []
    for i in range(0, col_devices, chunk):
        for k in range(i, i + chunk):
            m, g = spectra[0, k], spectra[1, k]
            mr, mi, gr, gi = m[:, :span], m[:, span:], g[:, :span], g[:, span:]
            both = jnp.concatenate([mr * gr + mi * gi, mr * gi - mi * gr], axis=0) * scale
            fsend[k] = both.astype(BF16)
        fcopy = pltpu.make_async_remote_copy(
            src_ref=fsend.at[pl.ds(i, chunk)],
            dst_ref=frecv.at[pl.ds(i, chunk)],
            send_sem=sf.at[i // chunk],
            recv_sem=rf.at[i // chunk],
            device_id={"dp": other_dp},
            device_id_type=MESH,
        )
        fcopy.start()
        fcopies.append(fcopy)

    loads[16].wait()
    back_stage(0)
    back_stage(1)

    loads[11].wait()
    fmcopies = []
    for i in range(0, col_devices, chunk):
        fcopies[i // chunk].wait_recv()
        some = pl.ds(i, chunk)
        both = fsend[some].astype(F32) + frecv[some].astype(F32)
        both = both.reshape(chunk * block, span).astype(BF16)
        fown[some] = both.reshape(chunk, block, span)
        both = jnp.dot(both, flip_lanes[...], preferred_element_type=F32).astype(BF16)
        for k in range(chunk):
            tile = both[k * block : (k + 1) * block]
            tile = jnp.dot(unflip_rows[...], tile, preferred_element_type=F32)
            fmsend[col_devices - 1 - i - k] = tile.astype(BF16)
        some = pl.ds(col_devices - i - chunk, chunk)
        fmcopy = pltpu.make_async_remote_copy(
            src_ref=fmsend.at[some],
            dst_ref=fmrecv.at[some],
            send_sem=sfm.at[i // chunk],
            recv_sem=rfm.at[i // chunk],
            device_id=partner,
            device_id_type=MESH,
        )
        fmcopy.start()
        fmcopies.append(fmcopy)

    def put(index, src, dst):
        copy = pltpu.make_async_copy(src, dst, out_sem.at[index])
        copy.start()
        return copy

    puts = []
    wait_recv(*row, 0, send4, recv4, s4, r4, 3)
    for c in range(row_devices):
        conv = recv4[0, c].astype(F32) + gain[c] * prod[0, c].astype(F32)
        grad_query[c] = (go[c].astype(F32) * conv).astype(BF16)
    puts.append(put(0, grad_query, grad_query_hbm))

    for k in reversed(range(col_devices)):
        if (k + 1) % chunk == 0:
            fmcopies[(col_devices - 1 - k) // chunk].wait_recv()
        mine, far = fown[k].astype(F32), fmrecv[k].astype(F32)
        pieces = []
        for p in range(2):
            near, rest = mine[p * act : (p + 1) * act], far[p * keep // 2 : (p + 1) * keep // 2]
            pieces += [near[: keep // 2], near[keep // 2 :] + rest[:8], rest[8:]]
        flip[pl.ds(k, span, stride=col_devices), : 2 * keep] = jnp.concatenate(pieces, axis=0).T
    for t in range(col_devices):
        lanes = slice(t * span, (t + 1) * span)
        tile = flip[lanes, : 2 * keep].T.astype(BF16)
        filter_grad[:, :, lanes] = tile.reshape(2, keep, span)
    puts.append(put(1, filter_grad, filter_grad_hbm))

    wait_recv(*row, 1, send4, recv4, s4, r4, 3)
    for c in range(row_devices):
        mixed_grad = recv4[1, c].astype(F32) + gain[c] * prod[1, c].astype(F32)
        grad_key[c] = (mixed_grad * vi[c].astype(F32)).astype(BF16)
        grad_value[c] = (mixed_grad * gk[c].astype(F32)).astype(BF16)
    puts.append(put(2, grad_key, grad_key_hbm))
    puts.append(put(3, grad_value, grad_value_hbm))

    for a in range(2):
        wait_send(*row, a, prod, recv1, s1, r1)
        wait_send(*col, a, send2, recv2, s2, r2)
        wait_send(*col, a, send3, recv3, s3, r3)
        wait_send(*row, a, send4, recv4, s4, r4)
    for copy in fcopies + fmcopies + [mirror]:
        copy.wait_send()
    for copy in puts:
        copy.wait()


def hand_over(*refs):
    sources, results, held, sems = refs[:4], refs[4:8], refs[8:12], refs[12]
    gets = [pltpu.make_async_copy(sources[i], held[i], sems.at[0, i]) for i in range(4)]
    puts = [pltpu.make_async_copy(held[i], results[i], sems.at[1, i]) for i in range(4)]
    for copy in gets:
        copy.start()
    for get, put in zip(gets, puts):
        get.wait()
        put.start()
    for copy in puts:
        copy.wait()


def shards(tables, row_devices, col_devices, gate_query, gate_key, value_input, grad_output, filter_spec, skip_gain):
    _, channels, rows_here, span = gate_query.shape
    keep = filter_spec.shape[2]
    cols_total = filter_spec.shape[3]
    rows_total = keep * col_devices
    half = rows_total // 2
    act = keep // 2 + 8
    dims = (row_devices, col_devices, keep, span, rows_here)
    anywhere = pl.BlockSpec(memory_space=pl.ANY)
    token = jax.ShapeDtypeStruct((channels, rows_here, span), BF16)
    names = [
        "forward_high", "forward_low", "inverse_rows", "twist", "place",
        "inner", "lane_high", "lane_low", "lane_inverse", "flip_lanes", "flip_rows",
        "unflip_rows",
    ]
    dma = pltpu.SemaphoreType.DMA
    tok = (2, row_devices, rows_here, span)
    mid = (2, col_devices, 2 * act, span)
    grad = (col_devices, 2 * act, span)
    mirrored = (col_devices, keep, span)
    freq = jax.ShapeDtypeStruct((2, keep, cols_total), BF16)
    chunks = (math.gcd(col_devices, 4),)
    chunks = (col_devices // chunks[0],)
    outs = pl.pallas_call(
        functools.partial(kernel, dims),
        out_shape=[token, token, token, freq],
        in_specs=[anywhere] * 5 + [pl.BlockSpec(memory_space=pltpu.SMEM)] + [anywhere] * len(names),
        out_specs=[anywhere] * 4,
        scratch_shapes=[pltpu.VMEM(token.shape, BF16)] * 4
        + [pltpu.VMEM(freq.shape, BF16)]
        + [pltpu.VMEM(tables[name].shape, tables[name].dtype) for name in names]
        + [pltpu.VMEM(token.shape, BF16)] * 3
        + [pltpu.VMEM(freq.shape, BF16)]
        + [
            pltpu.VMEM((cols_total, 128), F32),
            pltpu.VMEM(tok, BF16),
            pltpu.VMEM(tok, BF16),
            pltpu.VMEM(mid, BF16),
            pltpu.VMEM(mid, BF16),
            pltpu.VMEM(mid, BF16),
            pltpu.VMEM(mid, BF16),
            pltpu.VMEM(tok, BF16),
            pltpu.VMEM(tok, BF16),
            pltpu.VMEM(grad, F32),
            pltpu.VMEM((col_devices, act, 2 * span), F32),
            pltpu.VMEM((2, col_devices, act, 2 * span), F32),
            pltpu.VMEM((2, keep // 2, cols_total), BF16),
            pltpu.VMEM((2, col_devices, act, span), F32),
            pltpu.VMEM((2, col_devices, act, span), F32),
            pltpu.VMEM(grad, BF16),
            pltpu.VMEM(grad, BF16),
            pltpu.VMEM(grad, BF16),
            pltpu.VMEM(mirrored, BF16),
            pltpu.VMEM(mirrored, BF16),
            dma((17,)),
            dma((4,)),
            dma((4, 2)),
            dma((2, row_devices)), dma((2, row_devices)),
            dma((2, col_devices)), dma((2, col_devices)),
            dma((2, col_devices)), dma((2, col_devices)),
            dma((2, row_devices)), dma((2, row_devices)),
            dma(chunks), dma(chunks),
            dma(chunks), dma(chunks),
            dma, dma,
        ],
        compiler_params=pltpu.CompilerParams(
            collective_id=0, has_side_effects=True, vmem_limit_bytes=56 * 1024 * 1024
        ),
        name="hyena_backward",
    )(
        gate_query[0], gate_key[0], value_input[0], grad_output[0], filter_spec[:, 0], skip_gain,
        *[jnp.asarray(tables[name]) for name in names],
    )
    outs = pl.pallas_call(
        hand_over,
        out_shape=[jax.ShapeDtypeStruct(out.shape, out.dtype) for out in outs],
        in_specs=[anywhere] * 4,
        out_specs=[anywhere] * 4,
        scratch_shapes=[pltpu.VMEM(out.shape, out.dtype) for out in outs] + [dma((2, 4))],
        name="hand_over",
    )(*outs)
    return (outs[0][None], outs[1][None], outs[2][None], outs[3][:, None])


def solution(mesh):
    row_devices, col_devices = mesh.shape["row"], mesh.shape["col"]
    tokens = P("dp", None, "row", "col")
    freq = P(None, "row", "col", None)

    def run(gate_query, gate_key, value_input, grad_output, filter_spec, skip_gain):
        tables = make_tables(filter_spec.shape[2], filter_spec.shape[3], col_devices)
        return jax.shard_map(
            functools.partial(shards, tables, row_devices, col_devices),
            mesh=mesh,
            in_specs=(tokens, tokens, tokens, tokens, freq, P()),
            out_specs=(tokens, tokens, tokens, freq),
            check_vma=False,
        )(gate_query, gate_key, value_input, grad_output, filter_spec, skip_gain)

    return run
```

```python
import functools
import math

import jax
import jax.numpy as jnp
import numpy as np
from jax import lax
from jax.experimental import pallas as pl
from jax.experimental.pallas import tpu as pltpu
from jax.sharding import PartitionSpec as P

MESH = pl.DeviceIdType.MESH
BF16 = jnp.bfloat16
F32 = jnp.float32


def split_table(table):
    high = table.astype(np.float32).astype(BF16)
    low = (table - high.astype(np.float64)).astype(np.float32).astype(BF16)
    return high, low


def make_tables(rows_total, cols_total, col_devices):
    half = rows_total // 2
    span = cols_total // col_devices
    keep = rows_total // col_devices
    total = rows_total * cols_total
    act = keep // 2 + 8
    freq = keep * np.arange(col_devices)[:, None] + np.arange(act)
    angle = 2 * np.pi / rows_total * (freq[:, None, :, None] * np.arange(half) % rows_total)
    row_table = np.concatenate([np.cos(angle), -np.sin(angle)], axis=1)
    row_table[:, :, keep // 2 + 1 :] = 0
    row_table = row_table.reshape(col_devices * 2 * act, half)
    group = math.gcd(col_devices, 4)
    forward_high, forward_low = split_table(row_table.reshape(-1, group * 2 * act, half))
    inverse_rows = (row_table.T / total).astype(np.float32).astype(BF16)
    freq = freq.reshape(-1, 1)
    flip_lanes = np.eye(span)[::-1].astype(np.float32).astype(BF16)
    flip_rows = np.zeros((2, act, 2, keep // 2), np.float32)
    for r in range(1, keep // 2):
        flip_rows[0, r, 0, keep // 2 - r] = 1
        flip_rows[1, r, 1, keep // 2 - r] = -1
    flip_rows = flip_rows.reshape(2 * act, keep).astype(BF16)
    angle = 2 * np.pi / total * (freq * np.arange(span) % total)
    twist = np.stack([np.cos(angle), -np.sin(angle)]).astype(np.float32)
    lanes = np.arange(128)
    angle = 2 * np.pi / total * (freq * lanes * span % total)
    place = np.stack([np.cos(angle), -np.sin(angle)]).astype(np.float32)
    angle = 2 * np.pi / cols_total * (np.arange(col_devices)[:, None] * np.arange(span) % cols_total)
    inner = np.stack([np.cos(angle), -np.sin(angle)]).astype(np.float32)
    angle = 2 * np.pi / span * (np.arange(span)[:, None] * np.arange(span) % span)
    cosine, sine = np.cos(angle), np.sin(angle)
    lane_high, lane_low = split_table(np.block([[cosine, -sine], [sine, cosine]]))
    lane_inverse = np.block([[cosine, sine], [-sine, cosine]]).astype(np.float32).astype(BF16)
    return dict(
        forward_high=forward_high,
        forward_low=forward_low,
        inverse_rows=inverse_rows,
        twist=twist,
        place=place,
        inner=inner,
        lane_high=lane_high,
        lane_low=lane_low,
        lane_inverse=lane_inverse,
        flip_lanes=flip_lanes,
        flip_rows=flip_rows,
        unflip_rows=flip_rows.T,
    )


def times(a, b, cos_part, sin_part):
    return a * cos_part - b * sin_part, a * sin_part + b * cos_part


def small_fft(values, sign):
    n = len(values)
    if n == 1:
        return values
    if n == 2:
        (a, b), (c, d) = values
        return [(a + c, b + d), (a - c, b - d)]
    if n == 4:
        (a, b), (c, d), (e, f), (g, h) = values
        s0r, s0i, d0r, d0i = a + e, b + f, a - e, b - f
        s1r, s1i, d1r, d1i = c + g, d + h, c - g, d - h
        tr, ti = (-d1i, d1r) if sign > 0 else (d1i, -d1r)
        return [
            (s0r + s1r, s0i + s1i),
            (d0r + tr, d0i + ti),
            (s0r - s1r, s0i - s1i),
            (d0r - tr, d0i - ti),
        ]
    radix = 4 if n % 4 == 0 else 2
    other = n // radix
    out = [None] * n
    parts = []
    for b in range(radix):
        part = small_fft(values[b::radix], sign)
        turned = []
        for k, (re, im) in enumerate(part):
            turn = (b * k) % n
            if turn == 0:
                turned.append((re, im))
            elif 4 * turn == n:
                turned.append((-im, re) if sign > 0 else (im, -re))
            elif 8 * turn == n or 8 * turn == 3 * n:
                w = math.sqrt(0.5)
                c = w if 8 * turn == n else -w
                s = sign * w
                turned.append(times(re, im, c, s))
            else:
                angle = sign * 2 * math.pi * turn / n
                turned.append(times(re, im, math.cos(angle), math.sin(angle)))
        parts.append(turned)
    for k in range(other):
        column = small_fft([parts[b][k] for b in range(radix)], sign)
        for m in range(radix):
            out[k + other * m] = column[m]
    return out


def ring_order(size):
    return sorted(range(1, size), key=lambda s: -min(s, size - s))


def kernel(
    dims,
    gq_hbm, gk_hbm, vi_hbm, go_hbm, spec_hbm, gain,
    fwd_high_hbm, fwd_low_hbm, inv_hbm, twist_hbm, place_hbm, inner_hbm, lane_high_hbm, lane_low_hbm,
    lane_inv_hbm, flip_lanes_hbm, flip_rows_hbm, unflip_rows_hbm,
    grad_query_hbm, grad_key_hbm, grad_value_hbm, filter_grad_hbm,
    gq, gk, vi, go, spec,
    fwd_high, fwd_low, inv_rows, twist, place, inner, lane_high, lane_low,
    lane_inv, flip_lanes, flip_rows, unflip_rows,
    grad_query, grad_key, grad_value, filter_grad, flip,
    prod, recv1, send2, recv2, send3, recv3, send4, recv4,
    stage, wide, spectra, smir, sint, turned, fsend, frecv, fown, fmsend, fmrecv,
    load_sem, out_sem, own_sem, s1, r1, s2, r2, s3, r3, s4, r4, sf, rf, sfm, rfm, sm, rm,
):
    row_devices, col_devices, keep, span, rows_here = dims
    me_row = lax.axis_index("row")
    me_col = lax.axis_index("col")
    me_dp = lax.axis_index("dp")
    other_dp = 1 - me_dp
    act = keep // 2 + 8
    block = 2 * act
    rows_total = col_devices * keep
    half = rows_total // 2

    barrier = pltpu.get_barrier_semaphore()
    for s in range(1, row_devices):
        pl.semaphore_signal(
            barrier, inc=1, device_id={"row": lax.rem(me_row + s, row_devices)}, device_id_type=MESH
        )
    for s in range(1, col_devices):
        pl.semaphore_signal(
            barrier, inc=1, device_id={"col": lax.rem(me_col + s, col_devices)}, device_id_type=MESH
        )
    pl.semaphore_signal(barrier, inc=1, device_id={"dp": other_dp}, device_id_type=MESH)

    loads = [
        (gk_hbm, gk), (vi_hbm, vi), (go_hbm, go), (gq_hbm, gq), (spec_hbm, spec),
        (twist_hbm, twist), (place_hbm, place),
        (fwd_high_hbm, fwd_high), (fwd_low_hbm, fwd_low),
        (flip_lanes_hbm, flip_lanes), (flip_rows_hbm, flip_rows), (unflip_rows_hbm, unflip_rows),
        (inner_hbm, inner), (lane_high_hbm, lane_high), (lane_low_hbm, lane_low), (lane_inv_hbm, lane_inv),
        (inv_hbm, inv_rows),
    ]
    loads = [
        pltpu.make_async_copy(src, dst, load_sem.at[i]) for i, (src, dst) in enumerate(loads)
    ]
    for copy in loads:
        copy.start()

    def exchange(axis, me, size, a, send, recv, send_sem, recv_sem, index):
        return pltpu.make_async_remote_copy(
            src_ref=send.at[a, index],
            dst_ref=recv.at[a, me],
            send_sem=send_sem.at[a],
            recv_sem=recv_sem.at[a],
            device_id={axis: index},
            device_id_type=MESH,
        )

    def own(me, a, send, recv, step):
        return pltpu.make_async_copy(send.at[a, me], recv.at[a, me], own_sem.at[step, a])

    def wait_recv(axis, me, size, a, send, recv, send_sem, recv_sem, step):
        every = recv.at[a, pl.ds(0, size - 1)]
        pltpu.make_async_copy(every, every, recv_sem.at[a]).wait()
        own(me, a, send, recv, step).wait()

    def wait_send(axis, me, size, a, send, recv, send_sem, recv_sem):
        every = send.at[a, pl.ds(0, size - 1)]
        pltpu.make_async_copy(every, every, send_sem.at[a]).wait()

    row = ("row", me_row, row_devices)
    col = ("col", me_col, col_devices)

    for a, (left, right) in enumerate([(gk, vi), (go, gq)]):
        loads[2 * a].wait()
        loads[2 * a + 1].wait()
        prod[a] = (left[...].astype(F32) * right[...].astype(F32)).astype(BF16)
        if a == 0:
            pl.semaphore_wait(barrier, row_devices + col_devices - 1)
        for s in ring_order(row_devices):
            exchange(*row, a, prod, recv1, s1, r1, lax.rem(me_row + s, row_devices)).start()
        own(me_row, a, prod, recv1, 0).start()

    loads[4].wait()
    partner = {"col": col_devices - 1 - me_col}
    mirror = pltpu.make_async_remote_copy(
        src_ref=spec.at[:, pl.ds(keep // 2, keep // 2)],
        dst_ref=smir,
        send_sem=sm,
        recv_sem=rm,
        device_id=partner,
        device_id_type=MESH,
    )
    mirror.start()

    loads[5].wait()
    loads[6].wait()
    for c in range(col_devices):
        rows = pl.ds(c * act, act)
        lane = lax.broadcasted_iota(jnp.int32, (act, 128), 1) == me_col
        pr = jnp.sum(jnp.where(lane, place[0, rows], 0.0), axis=1, keepdims=True)
        pi = jnp.sum(jnp.where(lane, place[1, rows], 0.0), axis=1, keepdims=True)
        tr, ti = times(twist[0, rows], twist[1, rows], pr, pi)
        turned[0, c] = tr
        turned[1, c] = ti

    def spectrum_stage():
        mirror.wait_recv()
        loads[9].wait()
        loads[10].wait()
        for t in range(col_devices):
            lanes = slice(t * span, (t + 1) * span)
            far = slice((col_devices - 1 - t) * span, (col_devices - t) * span)
            got = smir[:, :, far].reshape(keep, span)
            got = jnp.dot(got, flip_lanes[...], preferred_element_type=F32).astype(BF16)
            got = jnp.dot(flip_rows[...], got, preferred_element_type=F32)
            tile = spec[:, :, lanes].astype(F32)[:, :act].reshape(block, span)
            flip[lanes, :block] = (tile + got).T
        for k in range(col_devices):
            tile = flip[pl.ds(k, span, stride=col_devices), :block].T
            sint[0, k] = tile[:act]
            sint[1, k] = tile[act:]

    def row_stage(a):
        wait_recv(*row, a, prod, recv1, s1, r1, 0)
        tokens = recv1[a].reshape(half, span)

        groups = fwd_high.shape[0]
        group = col_devices // groups

        def body(s, carry):
            g = lax.rem(lax.div(me_col, group) + 1 + s, groups)
            z = jnp.dot(fwd_high[g], tokens, preferred_element_type=F32)
            z = z + jnp.dot(fwd_low[g], tokens, preferred_element_type=F32)
            for i in range(group):
                d = g * group + i
                zr = z[i * block : i * block + act]
                zi = z[i * block + act : (i + 1) * block]
                re, im = times(zr, zi, turned[0, d], turned[1, d])
                send2[a, d] = jnp.concatenate([re, im], axis=0).astype(BF16)

                @pl.when(d != me_col)
                def _():
                    exchange(*col, a, send2, recv2, s2, r2, d).start()

            return carry

        lax.fori_loop(0, groups, body, 0)
        own(me_col, a, send2, recv2, 1).start()

    def col_stage(a):
        wait_recv(*col, a, send2, recv2, s2, r2, 1)

        def widen(c, carry):
            stage[c] = recv2[a, c].astype(F32)
            return carry

        lax.fori_loop(0, col_devices, widen, 0)

        def forward(t, carry):
            re_rows = pl.ds(pl.multiple_of(t * 8, 8), 8)
            im_rows = pl.ds(pl.multiple_of(act + t * 8, 8), 8)
            values = [(stage[c, re_rows], stage[c, im_rows]) for c in range(col_devices)]
            values = small_fft(values, -1)
            for k, (re, im) in enumerate(values):
                if k:
                    re, im = times(re, im, inner[0, k : k + 1], inner[1, k : k + 1])
                wide[k, re_rows, :span] = re
                wide[k, re_rows, span:] = im
            return carry

        lax.fori_loop(0, act // 8, forward, 0)

        group = math.gcd(col_devices, 8)

        def middle(g, carry):
            some = pl.ds(g * group, group)
            y = wide[some].reshape(group * act, 2 * span).astype(BF16)
            x = jnp.dot(y, lane_high[...], preferred_element_type=F32)
            x = x + jnp.dot(y, lane_low[...], preferred_element_type=F32)
            spectra[a, some] = x.reshape(group, act, 2 * span)
            sr = sint[0, some].reshape(group * act, span)
            si = sint[1, some].reshape(group * act, span)
            if a == 1:
                si = -si
            re, im = times(x[:, :span], x[:, span:], sr, si)
            v = jnp.concatenate([re, im], axis=1).astype(BF16)
            w = jnp.dot(v, lane_inv[...], preferred_element_type=F32)
            w = w.reshape(group, act, 2 * span)
            ir, ii = inner[0, some], inner[1, some]
            re, im = times(w[:, :, :span], w[:, :, span:], ir[:, None], -ii[:, None])
            wide[some, :, :span] = re
            wide[some, :, span:] = im
            return carry

        lax.fori_loop(0, col_devices // group, middle, 0)

        def backward(t, carry):
            re_rows = pl.ds(pl.multiple_of(t * 8, 8), 8)
            im_rows = pl.ds(pl.multiple_of(act + t * 8, 8), 8)
            values = [(wide[k, re_rows, :span], wide[k, re_rows, span:]) for k in range(col_devices)]
            values = small_fft(values, 1)
            for c, (re, im) in enumerate(values):
                stage[c, re_rows] = re
                stage[c, im_rows] = im
            return carry

        lax.fori_loop(0, act // 8, backward, 0)

        def narrow(s, carry):
            d = lax.rem(me_col + 1 + s, col_devices)
            send3[a, d] = stage[d].astype(BF16)

            @pl.when(s < col_devices - 1)
            def _():
                exchange(*col, a, send3, recv3, s3, r3, d).start()

            return carry

        lax.fori_loop(0, col_devices, narrow, 0)
        own(me_col, a, send3, recv3, 2).start()

    def back_stage(a):
        wait_recv(*col, a, send3, recv3, s3, r3, 2)
        parts = []
        for c in range(col_devices):
            got = recv3[a, c].astype(F32)
            re, im = times(got[:act], got[act:], turned[0, c], -turned[1, c])
            parts += [re, im]
        w = jnp.concatenate(parts, axis=0).astype(BF16)
        total = jnp.dot(inv_rows[...], w, preferred_element_type=F32)
        send4[a] = total.astype(BF16).reshape(row_devices, rows_here, span)
        for s in ring_order(row_devices):
            exchange(*row, a, send4, recv4, s4, r4, lax.rem(me_row + s, row_devices)).start()
        own(me_row, a, send4, recv4, 3).start()

    loads[7].wait()
    loads[8].wait()
    row_stage(0)
    spectrum_stage()
    row_stage(1)
    for i in range(12, 16):
        loads[i].wait()
    col_stage(0)
    col_stage(1)

    scale = 1.0 / (rows_total * col_devices * span)
    chunk = math.gcd(col_devices, 4)
    fcopies = []
    for i in range(0, col_devices, chunk):
        for k in range(i, i + chunk):
            m, g = spectra[0, k], spectra[1, k]
            mr, mi, gr, gi = m[:, :span], m[:, span:], g[:, :span], g[:, span:]
            both = jnp.concatenate([mr * gr + mi * gi, mr * gi - mi * gr], axis=0) * scale
            fsend[k] = both.astype(BF16)
        fcopy = pltpu.make_async_remote_copy(
            src_ref=fsend.at[pl.ds(i, chunk)],
            dst_ref=frecv.at[pl.ds(i, chunk)],
            send_sem=sf.at[i // chunk],
            recv_sem=rf.at[i // chunk],
            device_id={"dp": other_dp},
            device_id_type=MESH,
        )
        fcopy.start()
        fcopies.append(fcopy)

    loads[16].wait()
    back_stage(0)
    back_stage(1)

    loads[11].wait()
    fmcopies = []
    for i in range(0, col_devices, chunk):
        fcopies[i // chunk].wait_recv()
        some = pl.ds(i, chunk)
        both = fsend[some].astype(F32) + frecv[some].astype(F32)
        both = both.reshape(chunk * block, span).astype(BF16)
        fown[some] = both.reshape(chunk, block, span)
        both = jnp.dot(both, flip_lanes[...], preferred_element_type=F32).astype(BF16)
        for k in range(chunk):
            tile = both[k * block : (k + 1) * block]
            tile = jnp.dot(unflip_rows[...], tile, preferred_element_type=F32)
            fmsend[col_devices - 1 - i - k] = tile.astype(BF16)
        some = pl.ds(col_devices - i - chunk, chunk)
        fmcopy = pltpu.make_async_remote_copy(
            src_ref=fmsend.at[some],
            dst_ref=fmrecv.at[some],
            send_sem=sfm.at[i // chunk],
            recv_sem=rfm.at[i // chunk],
            device_id=partner,
            device_id_type=MESH,
        )
        fmcopy.start()
        fmcopies.append(fmcopy)

    def put(index, src, dst):
        copy = pltpu.make_async_copy(src, dst, out_sem.at[index])
        copy.start()
        return copy

    puts = []
    wait_recv(*row, 0, send4, recv4, s4, r4, 3)
    for c in range(row_devices):
        conv = recv4[0, c].astype(F32) + gain[c] * prod[0, c].astype(F32)
        grad_query[c] = (go[c].astype(F32) * conv).astype(BF16)
    puts.append(put(0, grad_query, grad_query_hbm))

    for k in reversed(range(col_devices)):
        if (k + 1) % chunk == 0:
            fmcopies[(col_devices - 1 - k) // chunk].wait_recv()
        mine, far = fown[k].astype(F32), fmrecv[k].astype(F32)
        pieces = []
        for p in range(2):
            near, rest = mine[p * act : (p + 1) * act], far[p * keep // 2 : (p + 1) * keep // 2]
            pieces += [near[: keep // 2], near[keep // 2 :] + rest[:8], rest[8:]]
        flip[pl.ds(k, span, stride=col_devices), : 2 * keep] = jnp.concatenate(pieces, axis=0).T
    for t in range(col_devices):
        lanes = slice(t * span, (t + 1) * span)
        tile = flip[lanes, : 2 * keep].T.astype(BF16)
        filter_grad[:, :, lanes] = tile.reshape(2, keep, span)
    puts.append(put(1, filter_grad, filter_grad_hbm))

    for a in range(2):
        wait_send(*row, a, prod, recv1, s1, r1)
        wait_send(*col, a, send2, recv2, s2, r2)
        wait_send(*col, a, send3, recv3, s3, r3)
    wait_recv(*row, 1, send4, recv4, s4, r4, 3)
    for c in range(row_devices):
        mixed_grad = recv4[1, c].astype(F32) + gain[c] * prod[1, c].astype(F32)
        grad_key[c] = (mixed_grad * vi[c].astype(F32)).astype(BF16)
        grad_value[c] = (mixed_grad * gk[c].astype(F32)).astype(BF16)
    puts.append(put(2, grad_key, grad_key_hbm))
    puts.append(put(3, grad_value, grad_value_hbm))

    for a in range(2):
        wait_send(*row, a, send4, recv4, s4, r4)
    for copy in fcopies + fmcopies + [mirror]:
        copy.wait_send()
    for copy in puts:
        copy.wait()


def hand_over(*refs):
    sources, results, held, sems = refs[:4], refs[4:8], refs[8:12], refs[12]
    gets = [pltpu.make_async_copy(sources[i], held[i], sems.at[0, i]) for i in range(4)]
    puts = [pltpu.make_async_copy(held[i], results[i], sems.at[1, i]) for i in range(4)]
    for copy in gets:
        copy.start()
    for get, put in zip(gets, puts):
        get.wait()
        put.start()
    for copy in puts:
        copy.wait()


def shards(tables, row_devices, col_devices, gate_query, gate_key, value_input, grad_output, filter_spec, skip_gain):
    _, channels, rows_here, span = gate_query.shape
    keep = filter_spec.shape[2]
    cols_total = filter_spec.shape[3]
    rows_total = keep * col_devices
    half = rows_total // 2
    act = keep // 2 + 8
    dims = (row_devices, col_devices, keep, span, rows_here)
    anywhere = pl.BlockSpec(memory_space=pl.ANY)
    token = jax.ShapeDtypeStruct((channels, rows_here, span), BF16)
    names = [
        "forward_high", "forward_low", "inverse_rows", "twist", "place",
        "inner", "lane_high", "lane_low", "lane_inverse", "flip_lanes", "flip_rows",
        "unflip_rows",
    ]
    dma = pltpu.SemaphoreType.DMA
    tok = (2, row_devices, rows_here, span)
    mid = (2, col_devices, 2 * act, span)
    grad = (col_devices, 2 * act, span)
    mirrored = (col_devices, keep, span)
    freq = jax.ShapeDtypeStruct((2, keep, cols_total), BF16)
    chunks = (math.gcd(col_devices, 4),)
    chunks = (col_devices // chunks[0],)
    outs = pl.pallas_call(
        functools.partial(kernel, dims),
        out_shape=[token, token, token, freq],
        in_specs=[anywhere] * 5 + [pl.BlockSpec(memory_space=pltpu.SMEM)] + [anywhere] * len(names),
        out_specs=[anywhere] * 4,
        scratch_shapes=[pltpu.VMEM(token.shape, BF16)] * 4
        + [pltpu.VMEM(freq.shape, BF16)]
        + [pltpu.VMEM(tables[name].shape, tables[name].dtype) for name in names]
        + [pltpu.VMEM(token.shape, BF16)] * 3
        + [pltpu.VMEM(freq.shape, BF16)]
        + [
            pltpu.VMEM((cols_total, 128), F32),
            pltpu.VMEM(tok, BF16),
            pltpu.VMEM(tok, BF16),
            pltpu.VMEM(mid, BF16),
            pltpu.VMEM(mid, BF16),
            pltpu.VMEM(mid, BF16),
            pltpu.VMEM(mid, BF16),
            pltpu.VMEM(tok, BF16),
            pltpu.VMEM(tok, BF16),
            pltpu.VMEM(grad, F32),
            pltpu.VMEM((col_devices, act, 2 * span), F32),
            pltpu.VMEM((2, col_devices, act, 2 * span), F32),
            pltpu.VMEM((2, keep // 2, cols_total), BF16),
            pltpu.VMEM((2, col_devices, act, span), F32),
            pltpu.VMEM((2, col_devices, act, span), F32),
            pltpu.VMEM(grad, BF16),
            pltpu.VMEM(grad, BF16),
            pltpu.VMEM(grad, BF16),
            pltpu.VMEM(mirrored, BF16),
            pltpu.VMEM(mirrored, BF16),
            dma((17,)),
            dma((4,)),
            dma((4, 2)),
            dma((2,)), dma((2,)), dma((2,)), dma((2,)), dma((2,)), dma((2,)), dma((2,)), dma((2,)),
            dma(chunks), dma(chunks),
            dma(chunks), dma(chunks),
            dma, dma,
        ],
        compiler_params=pltpu.CompilerParams(
            collective_id=0, has_side_effects=True, vmem_limit_bytes=56 * 1024 * 1024
        ),
        name="hyena_backward",
    )(
        gate_query[0], gate_key[0], value_input[0], grad_output[0], filter_spec[:, 0], skip_gain,
        *[jnp.asarray(tables[name]) for name in names],
    )
    outs = pl.pallas_call(
        hand_over,
        out_shape=[jax.ShapeDtypeStruct(out.shape, out.dtype) for out in outs],
        in_specs=[anywhere] * 4,
        out_specs=[anywhere] * 4,
        scratch_shapes=[pltpu.VMEM(out.shape, out.dtype) for out in outs] + [dma((2, 4))],
        name="hand_over",
    )(*outs)
    return (outs[0][None], outs[1][None], outs[2][None], outs[3][:, None])


def solution(mesh):
    row_devices, col_devices = mesh.shape["row"], mesh.shape["col"]
    tokens = P("dp", None, "row", "col")
    freq = P(None, "row", "col", None)

    def run(gate_query, gate_key, value_input, grad_output, filter_spec, skip_gain):
        tables = make_tables(filter_spec.shape[2], filter_spec.shape[3], col_devices)
        return jax.shard_map(
            functools.partial(shards, tables, row_devices, col_devices),
            mesh=mesh,
            in_specs=(tokens, tokens, tokens, tokens, freq, P()),
            out_specs=(tokens, tokens, tokens, freq),
            check_vma=False,
        )(gate_query, gate_key, value_input, grad_output, filter_spec, skip_gain)

    return run
```

```python
import functools
import math

import jax
import jax.numpy as jnp
import numpy as np
from jax import lax
from jax.experimental import pallas as pl
from jax.experimental.pallas import tpu as pltpu
from jax.sharding import PartitionSpec as P

MESH = pl.DeviceIdType.MESH
BF16 = jnp.bfloat16
F32 = jnp.float32


def split_table(table):
    high = table.astype(np.float32).astype(BF16)
    low = (table - high.astype(np.float64)).astype(np.float32).astype(BF16)
    return high, low


def make_tables(rows_total, cols_total, col_devices):
    half = rows_total // 2
    span = cols_total // col_devices
    keep = rows_total // col_devices
    total = rows_total * cols_total
    act, wire, middle = keep // 2 + 8, keep // 2, col_devices // 2
    freq = keep * np.arange(col_devices)[:, None] + np.arange(wire)
    freq[middle:] += 1
    angle = 2 * np.pi / rows_total * (freq[:, None, :, None] * np.arange(half) % rows_total)
    row_table = np.concatenate([np.cos(angle), -np.sin(angle)], axis=1)
    row_table[0, 1, 0] = 1.0 - 2.0 * (np.arange(half) % 2)
    row_table = row_table.reshape(col_devices * keep, half)
    group = math.gcd(col_devices, 4)
    forward_high, forward_low = split_table(row_table.reshape(-1, group * keep, half))
    inverse_rows = (row_table.T / total).astype(np.float32).astype(BF16)
    freq = freq.reshape(-1, 1)
    angle = np.pi / cols_total * np.arange(cols_total).reshape(col_devices, span)
    half_twist = np.stack([np.cos(angle), -np.sin(angle)]).astype(np.float32)
    flip_lanes = np.eye(span)[::-1].astype(np.float32).astype(BF16)
    own, mir = 0, 2 * keep
    pick = np.zeros((2, 2 * act, 2 * keep + 2 * wire), np.float32)
    unpick = np.zeros((2, 2 * wire + 16, 2 * wire), np.float32)
    merge = np.zeros((2, 2 * keep, 4 * wire), np.float32)
    for p, sign in enumerate((1, -1)):
        for i in range(wire):
            pick[0, p * act + i, own + p * keep + i] = 1
            pick[1, p * act + i, own + p * keep + i + 1] = 1
            pick[1, p * act + i, mir + p * wire + wire - 1 - i] = sign
            unpick[1, p * wire + wire - 1 - i, p * wire + i] = sign
            merge[0, p * keep + i, p * wire + i] = 1
            merge[0, p * keep + wire + i, 2 * wire + p * wire + i] = 1
            merge[1, p * keep + i + 1, p * wire + i] = 1
            if i:
                pick[0, p * act + i, mir + p * wire + wire - i] = sign
                unpick[0, p * wire + wire - i, p * wire + i] = sign
                merge[1, p * keep + wire + i, 2 * wire + p * wire + i] = 1
        unpick[0, 2 * wire + p, p * wire] = sign
    pick, unpick, merge = pick.astype(BF16), unpick.astype(BF16), merge.astype(BF16)
    angle = 2 * np.pi / total * (freq * np.arange(span) % total)
    twist = np.stack([np.cos(angle), -np.sin(angle)]).astype(np.float32)
    lanes = np.arange(128)
    angle = 2 * np.pi / total * (freq * lanes * span % total)
    place = np.stack([np.cos(angle), -np.sin(angle)]).astype(np.float32)
    angle = 2 * np.pi / cols_total * (np.arange(col_devices)[:, None] * np.arange(span) % cols_total)
    inner = np.stack([np.cos(angle), -np.sin(angle)]).astype(np.float32)
    angle = 2 * np.pi / span * (np.arange(span)[:, None] * np.arange(span) % span)
    cosine, sine = np.cos(angle), np.sin(angle)
    lane_high, lane_low = split_table(np.block([[cosine, -sine], [sine, cosine]]))
    lane_inverse = np.block([[cosine, sine], [-sine, cosine]]).astype(np.float32).astype(BF16)
    return dict(
        forward_high=forward_high,
        forward_low=forward_low,
        inverse_rows=inverse_rows,
        twist=twist,
        place=place,
        inner=inner,
        lane_high=lane_high,
        lane_low=lane_low,
        lane_inverse=lane_inverse,
        flip_lanes=flip_lanes,
        pick=pick,
        unpick=unpick,
        merge=merge,
        half_twist=half_twist,
    )


def times(a, b, cos_part, sin_part):
    return a * cos_part - b * sin_part, a * sin_part + b * cos_part


def small_fft(values, sign):
    n = len(values)
    if n == 1:
        return values
    if n == 2:
        (a, b), (c, d) = values
        return [(a + c, b + d), (a - c, b - d)]
    if n == 4:
        (a, b), (c, d), (e, f), (g, h) = values
        s0r, s0i, d0r, d0i = a + e, b + f, a - e, b - f
        s1r, s1i, d1r, d1i = c + g, d + h, c - g, d - h
        tr, ti = (-d1i, d1r) if sign > 0 else (d1i, -d1r)
        return [
            (s0r + s1r, s0i + s1i),
            (d0r + tr, d0i + ti),
            (s0r - s1r, s0i - s1i),
            (d0r - tr, d0i - ti),
        ]
    radix = 4 if n % 4 == 0 else 2
    other = n // radix
    out = [None] * n
    parts = []
    for b in range(radix):
        part = small_fft(values[b::radix], sign)
        turned = []
        for k, (re, im) in enumerate(part):
            turn = (b * k) % n
            if turn == 0:
                turned.append((re, im))
            elif 4 * turn == n:
                turned.append((-im, re) if sign > 0 else (im, -re))
            elif 8 * turn == n or 8 * turn == 3 * n:
                w = math.sqrt(0.5)
                c = w if 8 * turn == n else -w
                s = sign * w
                turned.append(times(re, im, c, s))
            else:
                angle = sign * 2 * math.pi * turn / n
                turned.append(times(re, im, math.cos(angle), math.sin(angle)))
        parts.append(turned)
    for k in range(other):
        column = small_fft([parts[b][k] for b in range(radix)], sign)
        for m in range(radix):
            out[k + other * m] = column[m]
    return out


def ring_order(size):
    return sorted(range(1, size), key=lambda s: -min(s, size - s))


def kernel(
    dims,
    gq_hbm, gk_hbm, vi_hbm, go_hbm, spec_hbm, gain,
    fwd_high_hbm, fwd_low_hbm, inv_hbm, twist_hbm, place_hbm, inner_hbm, lane_high_hbm, lane_low_hbm,
    lane_inv_hbm, flip_lanes_hbm, pick_hbm, unpick_hbm, merge_hbm, half_twist_hbm,
    grad_query_hbm, grad_key_hbm, grad_value_hbm, filter_grad_hbm,
    gq, gk, vi, go, spec,
    fwd_high, fwd_low, inv_rows, twist, place, inner, lane_high, lane_low,
    lane_inv, flip_lanes, pick, unpick, merge, half_twist,
    grad_query, grad_key, grad_value, filter_grad, flip,
    prod, recv1, send2, recv2, send3, recv3, send4, recv4,
    stage, wide, spectra, smir, sfar, head, sint, turned, fsend, frecv, fown, fmsend, fmrecv, extra, fx,
    load_sem, out_sem, own_sem, s1, r1, s2, r2, s3, r3, s4, r4, sf, rf, sfm, rfm, sx, rx,
):
    row_devices, col_devices, keep, span = dims
    me_row = lax.axis_index("row")
    me_col = lax.axis_index("col")
    me_dp = lax.axis_index("dp")
    other_dp = 1 - me_dp
    act = keep // 2 + 8
    wire = keep // 2
    block = 2 * act
    rows_total = col_devices * keep
    half = rows_total // 2

    barrier = pltpu.get_barrier_semaphore()
    for s in range(1, row_devices):
        pl.semaphore_signal(
            barrier, inc=1, device_id={"row": lax.rem(me_row + s, row_devices)}, device_id_type=MESH
        )
    for s in range(1, col_devices):
        pl.semaphore_signal(
            barrier, inc=1, device_id={"col": lax.rem(me_col + s, col_devices)}, device_id_type=MESH
        )
    partner = col_devices - 1 - me_col
    across = {"dp": other_dp, "col": partner}
    pl.semaphore_signal(barrier, inc=1, device_id={"dp": other_dp}, device_id_type=MESH)
    pl.semaphore_signal(barrier, inc=1, device_id=across, device_id_type=MESH)

    loads = [
        (gk_hbm, gk), (vi_hbm, vi), (go_hbm, go), (gq_hbm, gq), (spec_hbm, spec),
        (twist_hbm, twist), (place_hbm, place),
        (fwd_high_hbm, fwd_high), (fwd_low_hbm, fwd_low),
        (flip_lanes_hbm, flip_lanes), (pick_hbm, pick), (unpick_hbm, unpick),
        (inner_hbm, inner), (lane_high_hbm, lane_high), (lane_low_hbm, lane_low), (lane_inv_hbm, lane_inv),
        (inv_hbm, inv_rows), (merge_hbm, merge), (half_twist_hbm, half_twist),
    ]
    loads = [
        pltpu.make_async_copy(src, dst, load_sem.at[i]) for i, (src, dst) in enumerate(loads)
    ]
    for copy in loads:
        copy.start()

    def exchange(axis, me, size, a, send, recv, send_sem, recv_sem, index):
        return pltpu.make_async_remote_copy(
            src_ref=send.at[a, index],
            dst_ref=recv.at[a, me],
            send_sem=send_sem.at[a],
            recv_sem=recv_sem.at[a],
            device_id={axis: index},
            device_id_type=MESH,
        )

    def own(me, a, send, recv, step):
        return pltpu.make_async_copy(send.at[a, me], recv.at[a, me], own_sem.at[step, a])

    def wait_recv(axis, me, size, a, send, recv, send_sem, recv_sem, step):
        every = recv.at[a, pl.ds(0, size - 1)]
        pltpu.make_async_copy(every, every, recv_sem.at[a]).wait()
        own(me, a, send, recv, step).wait()

    def wait_send(axis, me, size, a, send, recv, send_sem, recv_sem):
        every = send.at[a, pl.ds(0, size - 1)]
        pltpu.make_async_copy(every, every, send_sem.at[a]).wait()

    row = ("row", me_row, row_devices)
    col = ("col", me_col, col_devices)

    for a, (left, right) in enumerate([(gk, vi), (go, gq)]):
        loads[2 * a].wait()
        loads[2 * a + 1].wait()
        prod[a] = (left[...].astype(F32) * right[...].astype(F32)).astype(BF16)
        if a == 0:
            pl.semaphore_wait(barrier, row_devices + col_devices)
        for s in ring_order(row_devices):
            exchange(*row, a, prod, recv1, s1, r1, lax.rem(me_row + s, row_devices)).start()
        own(me_row, a, prod, recv1, 0).start()

    loads[4].wait()
    middle = col_devices // 2
    side = lax.div(me_col, middle)
    other = jnp.where(lax.rem(me_col, middle) == 0, middle, col_devices) - me_col
    first = (me_col == 0).astype(F32)

    def send_one(src, dst, index, device):
        copy = pltpu.make_async_remote_copy(
            src_ref=src,
            dst_ref=dst,
            send_sem=sx.at[index],
            recv_sem=rx.at[index],
            device_id=device,
            device_id_type=MESH,
        )
        copy.start()
        return copy

    mirror = send_one(spec.at[:, pl.ds(wire, wire)], smir, 0, {"col": partner})
    for t in range(col_devices):
        heads = spec[:, :, t * span : (t + 1) * span].astype(F32)
        sfar[2 * t : 2 * t + 1] = heads[0, :1]
        sfar[2 * t + 1 : 2 * t + 2] = heads[1, :1]
    head[0] = sfar[...].astype(BF16)
    mirror_far = send_one(head.at[0], head.at[1], 1, {"col": other})

    loads[5].wait()
    loads[6].wait()
    for c in range(col_devices):
        rows = pl.ds(c * wire, wire)
        lane = lax.broadcasted_iota(jnp.int32, (wire, 128), 1) == me_col
        pr = jnp.sum(jnp.where(lane, place[0, rows], 0.0), axis=1, keepdims=True)
        pi = jnp.sum(jnp.where(lane, place[1, rows], 0.0), axis=1, keepdims=True)
        tr, ti = times(twist[0, rows], twist[1, rows], pr, pi)
        turned[0, c] = tr
        turned[1, c] = ti

    def spectrum_stage():
        mirror.wait_recv()
        mirror_far.wait_recv()
        loads[9].wait()
        loads[10].wait()
        low = 1.0 - first - side.astype(F32)
        sfar[...] = jnp.dot(head[1], flip_lanes[...], preferred_element_type=F32) * low
        heads = head[1].astype(F32) * first
        top = lax.broadcasted_iota(jnp.int32, (8, span), 0) == 0
        for t in range(col_devices):
            lanes = slice(t * span, (t + 1) * span)
            away = col_devices - 1 - t
            back = slice(away * span, (away + 1) * span)
            got = smir[:, :, back].reshape(2 * wire, span)
            got = jnp.dot(got, flip_lanes[...], preferred_element_type=F32).astype(BF16)
            tile = jnp.concatenate([spec[:, :, lanes].reshape(2 * keep, span), got], axis=0)
            tile = jnp.dot(pick[side], tile, preferred_element_type=F32)
            pieces = []
            for p, sign in enumerate((1.0, -1.0)):
                plane = tile[p * act : (p + 1) * act]
                turned_head = sign * sfar[2 * away + p : 2 * away + p + 1]
                pieces.append(jnp.where(top, plane[:8] + turned_head, plane[:8]))
                pieces.append(plane[8:wire])
                pieces.append(jnp.where(top, plane[wire:] + heads[2 * t + p : 2 * t + p + 1], plane[wire:]))
            flip[lanes, :block] = jnp.concatenate(pieces, axis=0).T
        for k in range(col_devices):
            tile = flip[pl.ds(k, span, stride=col_devices), :block].T
            sint[0, k] = tile[:act]
            sint[1, k] = tile[act:]

    def row_stage(a):
        wait_recv(*row, a, prod, recv1, s1, r1, 0)
        tokens = recv1[a].reshape(half, span)

        groups = fwd_high.shape[0]
        group = col_devices // groups

        def body(s, carry):
            g = lax.rem(lax.div(me_col, group) + 1 + s, groups)
            z = jnp.dot(fwd_high[g], tokens, preferred_element_type=F32)
            z = z + jnp.dot(fwd_low[g], tokens, preferred_element_type=F32)
            for i in range(group):
                d = g * group + i
                zr = z[i * keep : i * keep + wire]
                zi = z[i * keep + wire : (i + 1) * keep]
                re, im = times(zr, zi, turned[0, d], turned[1, d])
                send2[a, d] = jnp.concatenate([re, im], axis=0).astype(BF16)

                @pl.when(d != me_col)
                def _():
                    exchange(*col, a, send2, recv2, s2, r2, d).start()

            return carry

        lax.fori_loop(0, groups, body, 0)
        own(me_col, a, send2, recv2, 1).start()

    def col_stage(a):
        wait_recv(*col, a, send2, recv2, s2, r2, 1)

        def widen(c, carry):
            got = recv2[a, c].astype(F32)
            re, im = got[:wire], got[wire:]
            row_half = first * im[:1]
            top = lax.broadcasted_iota(jnp.int32, (8, span), 0) == 0
            stage[c, :wire] = re
            stage[c, wire:act] = jnp.where(top, row_half * half_twist[0, pl.ds(c, 1)], 0.0)
            stage[c, act : act + 8] = jnp.where(top, im[:8] - row_half, im[:8])
            stage[c, act + 8 : act + wire] = im[8:]
            stage[c, act + wire :] = jnp.where(top, row_half * half_twist[1, pl.ds(c, 1)], 0.0)
            return carry

        lax.fori_loop(0, col_devices, widen, 0)

        def forward(t, carry):
            re_rows = pl.ds(pl.multiple_of(t * 8, 8), 8)
            im_rows = pl.ds(pl.multiple_of(act + t * 8, 8), 8)
            values = [(stage[c, re_rows], stage[c, im_rows]) for c in range(col_devices)]
            values = small_fft(values, -1)
            for k, (re, im) in enumerate(values):
                if k:
                    re, im = times(re, im, inner[0, k : k + 1], inner[1, k : k + 1])
                wide[k, re_rows, :span] = re
                wide[k, re_rows, span:] = im
            return carry

        lax.fori_loop(0, act // 8, forward, 0)

        group = math.gcd(col_devices, 8)

        def middle(g, carry):
            some = pl.ds(g * group, group)
            y = wide[some].reshape(group * act, 2 * span).astype(BF16)
            x = jnp.dot(y, lane_high[...], preferred_element_type=F32)
            x = x + jnp.dot(y, lane_low[...], preferred_element_type=F32)
            spectra[a, some] = x.reshape(group, act, 2 * span)
            sr = sint[0, some].reshape(group * act, span)
            si = sint[1, some].reshape(group * act, span)
            if a == 1:
                si = -si
            re, im = times(x[:, :span], x[:, span:], sr, si)
            v = jnp.concatenate([re, im], axis=1).astype(BF16)
            w = jnp.dot(v, lane_inv[...], preferred_element_type=F32)
            w = w.reshape(group, act, 2 * span)
            ir, ii = inner[0, some], inner[1, some]
            re, im = times(w[:, :, :span], w[:, :, span:], ir[:, None], -ii[:, None])
            wide[some, :, :span] = re
            wide[some, :, span:] = im
            return carry

        lax.fori_loop(0, col_devices // group, middle, 0)

        def backward(t, carry):
            re_rows = pl.ds(pl.multiple_of(t * 8, 8), 8)
            im_rows = pl.ds(pl.multiple_of(act + t * 8, 8), 8)
            values = [(wide[k, re_rows, :span], wide[k, re_rows, span:]) for k in range(col_devices)]
            values = small_fft(values, 1)
            for c, (re, im) in enumerate(values):
                stage[c, re_rows] = re
                stage[c, im_rows] = im
            return carry

        lax.fori_loop(0, act // 8, backward, 0)

        def narrow(s, carry):
            d = lax.rem(me_col + 1 + s, col_devices)
            got = stage[d]
            re, im = got[:wire], got[act : act + wire]
            row_half = (
                got[wire : wire + 1] * half_twist[0, pl.ds(d, 1)]
                + got[act + wire : act + wire + 1] * half_twist[1, pl.ds(d, 1)]
            )
            top = lax.broadcasted_iota(jnp.int32, (wire, span), 0) == 0
            im = jnp.where(top, im + first * (row_half - im), im)
            send3[a, d] = jnp.concatenate([re, im], axis=0).astype(BF16)

            @pl.when(s < col_devices - 1)
            def _():
                exchange(*col, a, send3, recv3, s3, r3, d).start()

            return carry

        lax.fori_loop(0, col_devices, narrow, 0)
        own(me_col, a, send3, recv3, 2).start()

    def back_stage(a):
        wait_recv(*col, a, send3, recv3, s3, r3, 2)
        parts = []
        for c in range(col_devices):
            got = recv3[a, c].astype(F32)
            re, im = times(got[:wire], got[wire:], turned[0, c], -turned[1, c])
            parts += [re, im]
        w = jnp.concatenate(parts, axis=0).astype(BF16)
        total = jnp.dot(inv_rows[...], w, preferred_element_type=F32)
        send4[a] = total.astype(BF16).reshape(row_devices, half // row_devices, span)
        for s in ring_order(row_devices):
            exchange(*row, a, send4, recv4, s4, r4, lax.rem(me_row + s, row_devices)).start()
        own(me_row, a, send4, recv4, 3).start()

    loads[7].wait()
    loads[8].wait()
    row_stage(0)
    spectrum_stage()
    row_stage(1)
    for i in [12, 13, 14, 15, 18]:
        loads[i].wait()
    col_stage(0)
    col_stage(1)

    scale = 1.0 / (rows_total * col_devices * span)
    chunks = 4 if col_devices % 4 == 0 else 2
    chunk = col_devices // chunks

    def part(device, j):
        return lax.rem(device * (chunks // 2) + j, chunks)

    def fcopy(q):
        some = pl.ds(q * chunk, chunk)
        return pltpu.make_async_remote_copy(
            src_ref=fsend.at[some],
            dst_ref=frecv.at[some],
            send_sem=sf.at[q],
            recv_sem=rf.at[q],
            device_id={"dp": other_dp},
            device_id_type=MESH,
        )

    for j in range(chunks):
        q = part(other_dp, j)
        for i in range(chunk):
            k = q * chunk + i
            m, g = spectra[0, k], spectra[1, k]
            mr, mi, gr, gi = m[:, :span], m[:, span:], g[:, :span], g[:, span:]
            re, im = (mr * gr + mi * gi) * scale, (mr * gi - mi * gr) * scale
            fsend[k] = jnp.concatenate([re[:wire], im[:wire]], axis=0).astype(BF16)
            extra[pl.ds(2 * k, 1)] = re[wire : wire + 1]
            extra[pl.ds(2 * k + 1, 1)] = im[wire : wire + 1]
        fcopy(q).start()
    fx[0] = extra[...].astype(BF16)
    excopy = send_one(fx.at[0], fx.at[1], 3, {"dp": other_dp})

    loads[16].wait()
    back_stage(0)
    back_stage(1)

    loads[11].wait()
    def fmcopy(q, index, device):
        some = pl.ds((chunks - 1 - q) * chunk, chunk)
        return pltpu.make_async_remote_copy(
            src_ref=fmsend.at[some],
            dst_ref=fmrecv.at[some],
            send_sem=sfm.at[index],
            recv_sem=rfm.at[q],
            device_id=device,
            device_id_type=MESH,
        )

    fmcopies = []
    for j in range(chunks):
        q = part(me_dp, j)
        fcopy(q).wait_recv()
        some = pl.ds(q * chunk, chunk)
        both = fsend[some].astype(F32) + frecv[some].astype(F32)
        both = both.astype(BF16)
        fown[some] = both
        back = both.reshape(chunk * keep, span)
        back = jnp.dot(back, flip_lanes[...], preferred_element_type=F32).astype(BF16)
        for i in range(chunk):
            tile = back[i * keep : (i + 1) * keep]
            tile = jnp.dot(unpick[side], tile, preferred_element_type=F32)
            mirrored = col_devices - 1 - q * chunk - i
            fmsend[mirrored] = tile[:keep].astype(BF16)
            extra[pl.ds(2 * mirrored, 1)] = tile[keep : keep + 1]
            extra[pl.ds(2 * mirrored + 1, 1)] = tile[keep + 1 : keep + 2]
        if j < chunks // 2:
            for w, device in enumerate([across, {"col": partner}]):
                copy = fmcopy(q, 2 * j + w, device)
                copy.start()
                fmcopies.append(copy)
    excopy.wait_recv()
    both = fx[0].astype(F32) + fx[1].astype(F32)
    fx[2] = (extra[...] + first * (both - extra[...])).astype(BF16)
    fxcopy = send_one(fx.at[2], fx.at[3], 2, {"col": other})

    def put(index, src, dst):
        copy = pltpu.make_async_copy(src, dst, out_sem.at[index])
        copy.start()
        return copy

    puts = []
    wait_recv(*row, 0, send4, recv4, s4, r4, 3)
    for c in range(row_devices):
        conv = recv4[0, c].astype(F32) + gain[c] * prod[0, c].astype(F32)
        grad_query[c] = (go[c].astype(F32) * conv).astype(BF16)
    puts.append(put(0, grad_query, grad_query_hbm))

    fxcopy.wait_recv()
    extra[...] = fx[3].astype(F32) * side.astype(F32)
    top = lax.broadcasted_iota(jnp.int32, (8, span), 0) == 0
    loads[17].wait()
    for k in reversed(range(col_devices)):
        if (k + 1) % chunk == 0:
            fmcopy((col_devices - 1 - k) // chunk, 0, {"col": partner}).wait_recv()
        tile = jnp.concatenate([fown[k], fmrecv[k]], axis=0)
        tile = jnp.dot(merge[side], tile, preferred_element_type=F32)
        re = jnp.where(top, tile[:8] + extra[2 * k : 2 * k + 1], tile[:8])
        im = jnp.where(top, tile[keep : keep + 8] + extra[2 * k + 1 : 2 * k + 2], tile[keep : keep + 8])
        tile = jnp.concatenate([re, tile[8:keep], im, tile[keep + 8 :]], axis=0)
        flip[pl.ds(k, span, stride=col_devices), : 2 * keep] = tile.T
    for t in range(col_devices):
        lanes = slice(t * span, (t + 1) * span)
        tile = flip[lanes, : 2 * keep].T.astype(BF16)
        filter_grad[:, :, lanes] = tile.reshape(2, keep, span)
    puts.append(put(1, filter_grad, filter_grad_hbm))

    for a in range(2):
        wait_send(*row, a, prod, recv1, s1, r1)
        wait_send(*col, a, send2, recv2, s2, r2)
        wait_send(*col, a, send3, recv3, s3, r3)
    wait_recv(*row, 1, send4, recv4, s4, r4, 3)
    for c in range(row_devices):
        mixed_grad = recv4[1, c].astype(F32) + gain[c] * prod[1, c].astype(F32)
        grad_key[c] = (mixed_grad * vi[c].astype(F32)).astype(BF16)
        grad_value[c] = (mixed_grad * gk[c].astype(F32)).astype(BF16)
    puts.append(put(2, grad_key, grad_key_hbm))
    puts.append(put(3, grad_value, grad_value_hbm))

    for a in range(2):
        wait_send(*row, a, send4, recv4, s4, r4)
    for q in range(chunks):
        fcopy(q).wait_send()
    for copy in fmcopies + [mirror, mirror_far, excopy, fxcopy]:
        copy.wait_send()
    for copy in puts:
        copy.wait()


def hand_over(*refs):
    sources, results, held, sems = refs[:4], refs[4:8], refs[8:12], refs[12]
    gets = [pltpu.make_async_copy(sources[i], held[i], sems.at[0, i]) for i in range(4)]
    puts = [pltpu.make_async_copy(held[i], results[i], sems.at[1, i]) for i in range(4)]
    for copy in gets:
        copy.start()
    for get, put in zip(gets, puts):
        get.wait()
        put.start()
    for copy in puts:
        copy.wait()


def shards(tables, row_devices, col_devices, gate_query, gate_key, value_input, grad_output, filter_spec, skip_gain):
    _, channels, rows_here, span = gate_query.shape
    keep = filter_spec.shape[2]
    cols_total = filter_spec.shape[3]
    rows_total = keep * col_devices
    half = rows_total // 2
    act = keep // 2 + 8
    dims = (row_devices, col_devices, keep, span)
    anywhere = pl.BlockSpec(memory_space=pl.ANY)
    token = jax.ShapeDtypeStruct((channels, rows_here, span), BF16)
    names = [
        "forward_high", "forward_low", "inverse_rows", "twist", "place",
        "inner", "lane_high", "lane_low", "lane_inverse", "flip_lanes", "pick",
        "unpick", "merge", "half_twist",
    ]
    dma = pltpu.SemaphoreType.DMA
    tok = (2, row_devices, rows_here, span)
    mid = (2, col_devices, keep, span)
    grad = (col_devices, 2 * act, span)
    freq = jax.ShapeDtypeStruct((2, keep, cols_total), BF16)
    chunks = (4 if col_devices % 4 == 0 else 2,)
    outs = pl.pallas_call(
        functools.partial(kernel, dims),
        out_shape=[token, token, token, freq],
        in_specs=[anywhere] * 5 + [pl.BlockSpec(memory_space=pltpu.SMEM)] + [anywhere] * len(names),
        out_specs=[anywhere] * 4,
        scratch_shapes=[pltpu.VMEM(token.shape, BF16)] * 4
        + [pltpu.VMEM(freq.shape, BF16)]
        + [pltpu.VMEM(tables[name].shape, tables[name].dtype) for name in names]
        + [pltpu.VMEM(token.shape, BF16)] * 3
        + [pltpu.VMEM(freq.shape, BF16)]
        + [
            pltpu.VMEM((cols_total, 128), F32),
            pltpu.VMEM(tok, BF16),
            pltpu.VMEM(tok, BF16),
            pltpu.VMEM(mid, BF16),
            pltpu.VMEM(mid, BF16),
            pltpu.VMEM(mid, BF16),
            pltpu.VMEM(mid, BF16),
            pltpu.VMEM(tok, BF16),
            pltpu.VMEM(tok, BF16),
            pltpu.VMEM(grad, F32),
            pltpu.VMEM((col_devices, act, 2 * span), F32),
            pltpu.VMEM((2, col_devices, act, 2 * span), F32),
            pltpu.VMEM((2, keep // 2, cols_total), BF16),
            pltpu.VMEM((2 * col_devices, span), F32),
            pltpu.VMEM((2, 2 * col_devices, span), BF16),
            pltpu.VMEM((2, col_devices, act, span), F32),
            pltpu.VMEM((2, col_devices, keep // 2, span), F32),
            pltpu.VMEM(mid[1:], BF16),
            pltpu.VMEM(mid[1:], BF16),
            pltpu.VMEM(mid[1:], BF16),
            pltpu.VMEM(mid[1:], BF16),
            pltpu.VMEM(mid[1:], BF16),
            pltpu.VMEM((2 * col_devices, span), F32),
            pltpu.VMEM((4, 2 * col_devices, span), BF16),
            dma((19,)),
            dma((4,)),
            dma((4, 2)),
            dma((2,)), dma((2,)), dma((2,)), dma((2,)), dma((2,)), dma((2,)), dma((2,)), dma((2,)),
            dma(chunks), dma(chunks),
            dma(chunks), dma(chunks),
            dma((4,)), dma((4,)),
        ],
        compiler_params=pltpu.CompilerParams(
            collective_id=0, has_side_effects=True, vmem_limit_bytes=56 * 1024 * 1024
        ),
        name="hyena_backward",
    )(
        gate_query[0], gate_key[0], value_input[0], grad_output[0], filter_spec[:, 0], skip_gain,
        *[jnp.asarray(tables[name]) for name in names],
    )
    outs = pl.pallas_call(
        hand_over,
        out_shape=[jax.ShapeDtypeStruct(out.shape, out.dtype) for out in outs],
        in_specs=[anywhere] * 4,
        out_specs=[anywhere] * 4,
        scratch_shapes=[pltpu.VMEM(out.shape, out.dtype) for out in outs] + [dma((2, 4))],
        name="hand_over",
    )(*outs)
    return (outs[0][None], outs[1][None], outs[2][None], outs[3][:, None])


def solution(mesh):
    row_devices, col_devices = mesh.shape["row"], mesh.shape["col"]
    tokens = P("dp", None, "row", "col")
    freq = P(None, "row", "col", None)

    def run(gate_query, gate_key, value_input, grad_output, filter_spec, skip_gain):
        tables = make_tables(filter_spec.shape[2], filter_spec.shape[3], col_devices)
        return jax.shard_map(
            functools.partial(shards, tables, row_devices, col_devices),
            mesh=mesh,
            in_specs=(tokens, tokens, tokens, tokens, freq, P()),
            out_specs=(tokens, tokens, tokens, freq),
            check_vma=False,
        )(gate_query, gate_key, value_input, grad_output, filter_spec, skip_gain)

    return run
```

```python
import functools
import math

import jax
import jax.numpy as jnp
import numpy as np
from jax import lax
from jax.experimental import pallas as pl
from jax.experimental.pallas import tpu as pltpu
from jax.sharding import PartitionSpec as P

MESH = pl.DeviceIdType.MESH
BF16 = jnp.bfloat16
F32 = jnp.float32


def split_table(table):
    high = table.astype(np.float32).astype(BF16)
    low = (table - high.astype(np.float64)).astype(np.float32).astype(BF16)
    return high, low


def make_tables(rows_total, cols_total, col_devices):
    half = rows_total // 2
    span = cols_total // col_devices
    keep = rows_total // col_devices
    total = rows_total * cols_total
    act, wire, middle = keep // 2 + 8, keep // 2, col_devices // 2
    freq = keep * np.arange(col_devices)[:, None] + np.arange(wire)
    freq[middle:] += 1
    angle = 2 * np.pi / rows_total * (freq[:, None, :, None] * np.arange(half) % rows_total)
    row_table = np.concatenate([np.cos(angle), -np.sin(angle)], axis=1)
    row_table[0, 1, 0] = 1.0 - 2.0 * (np.arange(half) % 2)
    row_table = row_table.reshape(col_devices * keep, half)
    group = math.gcd(col_devices, 4)
    forward_high, forward_low = split_table(row_table.reshape(-1, group * keep, half))
    inverse_rows = (row_table.T / total).astype(np.float32).astype(BF16)
    freq = freq.reshape(-1, 1)
    angle = np.pi / cols_total * np.arange(cols_total).reshape(col_devices, span)
    half_twist = np.stack([np.cos(angle), -np.sin(angle)]).astype(np.float32)
    flip_lanes = np.eye(span)[::-1].astype(np.float32).astype(BF16)
    own, mir = 0, 2 * keep
    pick = np.zeros((2, 2 * act, 2 * keep + 2 * wire), np.float32)
    unpick = np.zeros((2, 2 * wire + 16, 2 * wire), np.float32)
    merge = np.zeros((2, 2 * keep, 4 * wire), np.float32)
    for p, sign in enumerate((1, -1)):
        for i in range(wire):
            pick[0, p * act + i, own + p * keep + i] = 1
            pick[1, p * act + i, own + p * keep + i + 1] = 1
            pick[1, p * act + i, mir + p * wire + wire - 1 - i] = sign
            unpick[1, p * wire + wire - 1 - i, p * wire + i] = sign
            merge[0, p * keep + i, p * wire + i] = 1
            merge[0, p * keep + wire + i, 2 * wire + p * wire + i] = 1
            merge[1, p * keep + i + 1, p * wire + i] = 1
            if i:
                pick[0, p * act + i, mir + p * wire + wire - i] = sign
                unpick[0, p * wire + wire - i, p * wire + i] = sign
                merge[1, p * keep + wire + i, 2 * wire + p * wire + i] = 1
        unpick[0, 2 * wire + p, p * wire] = sign
    pick, unpick, merge = pick.astype(BF16), unpick.astype(BF16), merge.astype(BF16)
    angle = 2 * np.pi / total * (freq * np.arange(span) % total)
    twist = np.stack([np.cos(angle), -np.sin(angle)]).astype(np.float32)
    lanes = np.arange(128)
    angle = 2 * np.pi / total * (freq * lanes * span % total)
    place = np.stack([np.cos(angle), -np.sin(angle)]).astype(np.float32)
    angle = 2 * np.pi / cols_total * (np.arange(col_devices)[:, None] * np.arange(span) % cols_total)
    inner = np.stack([np.cos(angle), -np.sin(angle)]).astype(np.float32)
    angle = 2 * np.pi / span * (np.arange(span)[:, None] * np.arange(span) % span)
    cosine, sine = np.cos(angle), np.sin(angle)
    lane_high, lane_low = split_table(np.block([[cosine, -sine], [sine, cosine]]))
    lane_inverse = np.block([[cosine, sine], [-sine, cosine]]).astype(np.float32).astype(BF16)
    return dict(
        forward_high=forward_high,
        forward_low=forward_low,
        inverse_rows=inverse_rows,
        twist=twist,
        place=place,
        inner=inner,
        lane_high=lane_high,
        lane_low=lane_low,
        lane_inverse=lane_inverse,
        flip_lanes=flip_lanes,
        pick=pick,
        unpick=unpick,
        merge=merge,
        half_twist=half_twist,
    )


def times(a, b, cos_part, sin_part):
    return a * cos_part - b * sin_part, a * sin_part + b * cos_part


def small_fft(values, sign):
    n = len(values)
    if n == 1:
        return values
    if n == 2:
        (a, b), (c, d) = values
        return [(a + c, b + d), (a - c, b - d)]
    if n == 4:
        (a, b), (c, d), (e, f), (g, h) = values
        s0r, s0i, d0r, d0i = a + e, b + f, a - e, b - f
        s1r, s1i, d1r, d1i = c + g, d + h, c - g, d - h
        tr, ti = (-d1i, d1r) if sign > 0 else (d1i, -d1r)
        return [
            (s0r + s1r, s0i + s1i),
            (d0r + tr, d0i + ti),
            (s0r - s1r, s0i - s1i),
            (d0r - tr, d0i - ti),
        ]
    radix = 4 if n % 4 == 0 else 2
    other = n // radix
    out = [None] * n
    parts = []
    for b in range(radix):
        part = small_fft(values[b::radix], sign)
        turned = []
        for k, (re, im) in enumerate(part):
            turn = (b * k) % n
            if turn == 0:
                turned.append((re, im))
            elif 4 * turn == n:
                turned.append((-im, re) if sign > 0 else (im, -re))
            elif 8 * turn == n or 8 * turn == 3 * n:
                w = math.sqrt(0.5)
                c = w if 8 * turn == n else -w
                s = sign * w
                turned.append(times(re, im, c, s))
            else:
                angle = sign * 2 * math.pi * turn / n
                turned.append(times(re, im, math.cos(angle), math.sin(angle)))
        parts.append(turned)
    for k in range(other):
        column = small_fft([parts[b][k] for b in range(radix)], sign)
        for m in range(radix):
            out[k + other * m] = column[m]
    return out


def far_first(size, send):
    def body(i, carry):
        send(size // 2 + lax.div(i + 1, 2) * (1 - 2 * lax.rem(i, 2)))
        return carry

    lax.fori_loop(0, size - 1, body, 0)


def kernel(
    dims,
    gq_hbm, gk_hbm, vi_hbm, go_hbm, spec_hbm, gain,
    fwd_high_hbm, fwd_low_hbm, inv_hbm, twist_hbm, place_hbm, inner_hbm, lane_high_hbm, lane_low_hbm,
    lane_inv_hbm, flip_lanes_hbm, pick_hbm, unpick_hbm, merge_hbm, half_twist_hbm,
    grad_query_hbm, grad_key_hbm, grad_value_hbm, filter_grad_hbm,
    gq, gk, vi, go, spec,
    fwd_high, fwd_low, inv_rows, twist, place, inner, lane_high, lane_low,
    lane_inv, flip_lanes, pick, unpick, merge, half_twist,
    grad_query, grad_key, grad_value, filter_grad, flip,
    prod, recv1, send2, recv2, send3, recv3, send4, recv4,
    stage, wide, spectra, smir, sfar, head, sint, turned, fsend, frecv, fown, fmsend, fmrecv, extra, fx,
    load_sem, out_sem, own_sem, s1, r1, s2, r2, s3, r3, s4, r4, sf, rf, sfm, rfm, sx, rx,
):
    row_devices, col_devices, keep, span = dims
    me_row = lax.axis_index("row")
    me_col = lax.axis_index("col")
    me_dp = lax.axis_index("dp")
    other_dp = 1 - me_dp
    act = keep // 2 + 8
    wire = keep // 2
    block = 2 * act
    rows_total = col_devices * keep
    half = rows_total // 2

    barrier = pltpu.get_barrier_semaphore()
    for s in range(1, row_devices):
        pl.semaphore_signal(
            barrier, inc=1, device_id={"row": lax.rem(me_row + s, row_devices)}, device_id_type=MESH
        )
    for s in range(1, col_devices):
        pl.semaphore_signal(
            barrier, inc=1, device_id={"col": lax.rem(me_col + s, col_devices)}, device_id_type=MESH
        )
    partner = col_devices - 1 - me_col
    across = {"dp": other_dp, "col": partner}
    pl.semaphore_signal(barrier, inc=1, device_id={"dp": other_dp}, device_id_type=MESH)
    pl.semaphore_signal(barrier, inc=1, device_id=across, device_id_type=MESH)

    loads = [
        (gk_hbm, gk), (vi_hbm, vi), (go_hbm, go), (gq_hbm, gq), (spec_hbm, spec),
        (twist_hbm, twist), (place_hbm, place),
        (fwd_high_hbm, fwd_high), (fwd_low_hbm, fwd_low),
        (flip_lanes_hbm, flip_lanes), (pick_hbm, pick), (unpick_hbm, unpick),
        (inner_hbm, inner), (lane_high_hbm, lane_high), (lane_low_hbm, lane_low), (lane_inv_hbm, lane_inv),
        (inv_hbm, inv_rows), (merge_hbm, merge), (half_twist_hbm, half_twist),
    ]
    loads = [
        pltpu.make_async_copy(src, dst, load_sem.at[i]) for i, (src, dst) in enumerate(loads)
    ]
    for copy in loads:
        copy.start()

    def exchange(axis, me, size, a, send, recv, send_sem, recv_sem, index):
        return pltpu.make_async_remote_copy(
            src_ref=send.at[a, index],
            dst_ref=recv.at[a, me],
            send_sem=send_sem.at[a],
            recv_sem=recv_sem.at[a],
            device_id={axis: index},
            device_id_type=MESH,
        )

    def own(me, a, send, recv, step):
        return pltpu.make_async_copy(send.at[a, me], recv.at[a, me], own_sem.at[step, a])

    def wait_recv(axis, me, size, a, send, recv, send_sem, recv_sem, step):
        every = recv.at[a, pl.ds(0, size - 1)]
        pltpu.make_async_copy(every, every, recv_sem.at[a]).wait()
        own(me, a, send, recv, step).wait()

    def wait_send(axis, me, size, a, send, recv, send_sem, recv_sem):
        every = send.at[a, pl.ds(0, size - 1)]
        pltpu.make_async_copy(every, every, send_sem.at[a]).wait()

    row = ("row", me_row, row_devices)
    col = ("col", me_col, col_devices)

    for a, (left, right) in enumerate([(gk, vi), (go, gq)]):
        loads[2 * a].wait()
        loads[2 * a + 1].wait()
        prod[a] = (left[...].astype(F32) * right[...].astype(F32)).astype(BF16)
        if a == 0:
            pl.semaphore_wait(barrier, row_devices + col_devices)
        far_first(
            row_devices,
            lambda s: exchange(*row, a, prod, recv1, s1, r1, lax.rem(me_row + s, row_devices)).start(),
        )
        own(me_row, a, prod, recv1, 0).start()

    loads[4].wait()
    middle = col_devices // 2
    side = lax.div(me_col, middle)
    other = jnp.where(lax.rem(me_col, middle) == 0, middle, col_devices) - me_col
    first = (me_col == 0).astype(F32)

    def send_one(src, dst, index, device):
        copy = pltpu.make_async_remote_copy(
            src_ref=src,
            dst_ref=dst,
            send_sem=sx.at[index],
            recv_sem=rx.at[index],
            device_id=device,
            device_id_type=MESH,
        )
        copy.start()
        return copy

    mirror = send_one(spec.at[:, pl.ds(wire, wire)], smir, 0, {"col": partner})
    for t in range(col_devices):
        heads = spec[:, :, t * span : (t + 1) * span].astype(F32)
        sfar[2 * t : 2 * t + 1] = heads[0, :1]
        sfar[2 * t + 1 : 2 * t + 2] = heads[1, :1]
    head[0] = sfar[...].astype(BF16)
    mirror_far = send_one(head.at[0], head.at[1], 1, {"col": other})

    loads[5].wait()
    loads[6].wait()
    @pl.loop(0, col_devices)
    def _(c):
        rows = pl.ds(pl.multiple_of(c * wire, wire), wire)
        lane = lax.broadcasted_iota(jnp.int32, (wire, 128), 1) == me_col
        pr = jnp.sum(jnp.where(lane, place[0, rows], 0.0), axis=1, keepdims=True)
        pi = jnp.sum(jnp.where(lane, place[1, rows], 0.0), axis=1, keepdims=True)
        tr, ti = times(twist[0, rows], twist[1, rows], pr, pi)
        turned[0, c] = tr
        turned[1, c] = ti

    def spectrum_stage():
        mirror.wait_recv()
        mirror_far.wait_recv()
        loads[9].wait()
        loads[10].wait()
        low = 1.0 - first - side.astype(F32)
        sfar[...] = jnp.dot(head[1], flip_lanes[...], preferred_element_type=F32) * low
        heads = head[1].astype(F32) * first
        top = lax.broadcasted_iota(jnp.int32, (8, span), 0) == 0
        for t in range(col_devices):
            lanes = slice(t * span, (t + 1) * span)
            away = col_devices - 1 - t
            back = slice(away * span, (away + 1) * span)
            got = smir[:, :, back].reshape(2 * wire, span)
            got = jnp.dot(got, flip_lanes[...], preferred_element_type=F32).astype(BF16)
            tile = jnp.concatenate([spec[:, :, lanes].reshape(2 * keep, span), got], axis=0)
            tile = jnp.dot(pick[side], tile, preferred_element_type=F32)
            pieces = []
            for p, sign in enumerate((1.0, -1.0)):
                plane = tile[p * act : (p + 1) * act]
                turned_head = sign * sfar[2 * away + p : 2 * away + p + 1]
                pieces.append(jnp.where(top, plane[:8] + turned_head, plane[:8]))
                pieces.append(plane[8:wire])
                pieces.append(jnp.where(top, plane[wire:] + heads[2 * t + p : 2 * t + p + 1], plane[wire:]))
            flip[lanes, :block] = jnp.concatenate(pieces, axis=0).T
        for k in range(col_devices):
            tile = flip[pl.ds(k, span, stride=col_devices), :block].T
            sint[0, k] = tile[:act]
            sint[1, k] = tile[act:]

    def row_stage(a):
        wait_recv(*row, a, prod, recv1, s1, r1, 0)
        tokens = recv1[a].reshape(half, span)

        groups = fwd_high.shape[0]
        group = col_devices // groups

        def body(s, carry):
            g = lax.rem(lax.div(me_col, group) + 1 + s, groups)
            z = jnp.dot(fwd_high[g], tokens, preferred_element_type=F32)
            z = z + jnp.dot(fwd_low[g], tokens, preferred_element_type=F32)
            for i in range(group):
                d = g * group + i
                zr = z[i * keep : i * keep + wire]
                zi = z[i * keep + wire : (i + 1) * keep]
                re, im = times(zr, zi, turned[0, d], turned[1, d])
                send2[a, d] = jnp.concatenate([re, im], axis=0).astype(BF16)

                @pl.when(d != me_col)
                def _():
                    exchange(*col, a, send2, recv2, s2, r2, d).start()

            return carry

        lax.fori_loop(0, groups, body, 0)
        own(me_col, a, send2, recv2, 1).start()

    def col_stage(a):
        wait_recv(*col, a, send2, recv2, s2, r2, 1)

        def widen(c, carry):
            got = recv2[a, c].astype(F32)
            re, im = got[:wire], got[wire:]
            row_half = first * im[:1]
            top = lax.broadcasted_iota(jnp.int32, (8, span), 0) == 0
            stage[c, :wire] = re
            stage[c, wire:act] = jnp.where(top, row_half * half_twist[0, pl.ds(c, 1)], 0.0)
            stage[c, act : act + 8] = jnp.where(top, im[:8] - row_half, im[:8])
            stage[c, act + 8 : act + wire] = im[8:]
            stage[c, act + wire :] = jnp.where(top, row_half * half_twist[1, pl.ds(c, 1)], 0.0)
            return carry

        lax.fori_loop(0, col_devices, widen, 0)

        def forward(t, carry):
            re_rows = pl.ds(pl.multiple_of(t * 8, 8), 8)
            im_rows = pl.ds(pl.multiple_of(act + t * 8, 8), 8)
            values = [(stage[c, re_rows], stage[c, im_rows]) for c in range(col_devices)]
            values = small_fft(values, -1)
            for k, (re, im) in enumerate(values):
                if k:
                    re, im = times(re, im, inner[0, k : k + 1], inner[1, k : k + 1])
                wide[k, re_rows, :span] = re
                wide[k, re_rows, span:] = im
            return carry

        lax.fori_loop(0, act // 8, forward, 0)

        group = math.gcd(col_devices, 8)

        def middle(g, carry):
            some = pl.ds(g * group, group)
            y = wide[some].reshape(group * act, 2 * span).astype(BF16)
            x = jnp.dot(y, lane_high[...], preferred_element_type=F32)
            x = x + jnp.dot(y, lane_low[...], preferred_element_type=F32)
            spectra[a, some] = x.reshape(group, act, 2 * span)
            sr = sint[0, some].reshape(group * act, span)
            si = sint[1, some].reshape(group * act, span)
            if a == 1:
                si = -si
            re, im = times(x[:, :span], x[:, span:], sr, si)
            v = jnp.concatenate([re, im], axis=1).astype(BF16)
            w = jnp.dot(v, lane_inv[...], preferred_element_type=F32)
            w = w.reshape(group, act, 2 * span)
            ir, ii = inner[0, some], inner[1, some]
            re, im = times(w[:, :, :span], w[:, :, span:], ir[:, None], -ii[:, None])
            wide[some, :, :span] = re
            wide[some, :, span:] = im
            return carry

        lax.fori_loop(0, col_devices // group, middle, 0)

        def backward(t, carry):
            re_rows = pl.ds(pl.multiple_of(t * 8, 8), 8)
            im_rows = pl.ds(pl.multiple_of(act + t * 8, 8), 8)
            values = [(wide[k, re_rows, :span], wide[k, re_rows, span:]) for k in range(col_devices)]
            values = small_fft(values, 1)
            for c, (re, im) in enumerate(values):
                stage[c, re_rows] = re
                stage[c, im_rows] = im
            return carry

        lax.fori_loop(0, act // 8, backward, 0)

        def narrow(s, carry):
            d = lax.rem(me_col + 1 + s, col_devices)
            got = stage[d]
            re, im = got[:wire], got[act : act + wire]
            row_half = (
                got[wire : wire + 1] * half_twist[0, pl.ds(d, 1)]
                + got[act + wire : act + wire + 1] * half_twist[1, pl.ds(d, 1)]
            )
            top = lax.broadcasted_iota(jnp.int32, (wire, span), 0) == 0
            im = jnp.where(top, im + first * (row_half - im), im)
            send3[a, d] = jnp.concatenate([re, im], axis=0).astype(BF16)

            @pl.when(s < col_devices - 1)
            def _():
                exchange(*col, a, send3, recv3, s3, r3, d).start()

            return carry

        lax.fori_loop(0, col_devices, narrow, 0)
        own(me_col, a, send3, recv3, 2).start()

    def back_stage(a):
        wait_recv(*col, a, send3, recv3, s3, r3, 2)
        parts = []
        for c in range(col_devices):
            got = recv3[a, c].astype(F32)
            re, im = times(got[:wire], got[wire:], turned[0, c], -turned[1, c])
            parts += [re, im]
        w = jnp.concatenate(parts, axis=0).astype(BF16)
        total = jnp.dot(inv_rows[...], w, preferred_element_type=F32)
        send4[a] = total.astype(BF16).reshape(row_devices, half // row_devices, span)
        far_first(
            row_devices,
            lambda s: exchange(*row, a, send4, recv4, s4, r4, lax.rem(me_row + s, row_devices)).start(),
        )
        own(me_row, a, send4, recv4, 3).start()

    loads[7].wait()
    loads[8].wait()
    row_stage(0)
    spectrum_stage()
    row_stage(1)
    for i in [12, 13, 14, 15, 18]:
        loads[i].wait()
    col_stage(0)
    col_stage(1)

    scale = 1.0 / (rows_total * col_devices * span)
    chunks = 4 if col_devices % 4 == 0 else 2
    chunk = col_devices // chunks

    def part(device, j):
        return lax.rem(device * (chunks // 2) + j, chunks)

    def fcopy(q):
        some = pl.ds(q * chunk, chunk)
        return pltpu.make_async_remote_copy(
            src_ref=fsend.at[some],
            dst_ref=frecv.at[some],
            send_sem=sf.at[q],
            recv_sem=rf.at[q],
            device_id={"dp": other_dp},
            device_id_type=MESH,
        )

    for j in range(chunks):
        q = part(other_dp, j)
        for i in range(chunk):
            k = q * chunk + i
            m, g = spectra[0, k], spectra[1, k]
            mr, mi, gr, gi = m[:, :span], m[:, span:], g[:, :span], g[:, span:]
            re, im = (mr * gr + mi * gi) * scale, (mr * gi - mi * gr) * scale
            fsend[k] = jnp.concatenate([re[:wire], im[:wire]], axis=0).astype(BF16)
            extra[pl.ds(2 * k, 1)] = re[wire : wire + 1]
            extra[pl.ds(2 * k + 1, 1)] = im[wire : wire + 1]
        fcopy(q).start()
    fx[0] = extra[...].astype(BF16)
    excopy = send_one(fx.at[0], fx.at[1], 3, {"dp": other_dp})

    loads[16].wait()
    back_stage(0)
    back_stage(1)

    loads[11].wait()
    def fmcopy(q, index, device):
        some = pl.ds((chunks - 1 - q) * chunk, chunk)
        return pltpu.make_async_remote_copy(
            src_ref=fmsend.at[some],
            dst_ref=fmrecv.at[some],
            send_sem=sfm.at[index],
            recv_sem=rfm.at[q],
            device_id=device,
            device_id_type=MESH,
        )

    fmcopies = []
    for j in range(chunks):
        q = part(me_dp, j)
        fcopy(q).wait_recv()
        some = pl.ds(q * chunk, chunk)
        both = fsend[some].astype(F32) + frecv[some].astype(F32)
        both = both.astype(BF16)
        fown[some] = both
        back = both.reshape(chunk * keep, span)
        back = jnp.dot(back, flip_lanes[...], preferred_element_type=F32).astype(BF16)
        for i in range(chunk):
            tile = back[i * keep : (i + 1) * keep]
            tile = jnp.dot(unpick[side], tile, preferred_element_type=F32)
            mirrored = col_devices - 1 - q * chunk - i
            fmsend[mirrored] = tile[:keep].astype(BF16)
            extra[pl.ds(2 * mirrored, 1)] = tile[keep : keep + 1]
            extra[pl.ds(2 * mirrored + 1, 1)] = tile[keep + 1 : keep + 2]
        if j < chunks // 2:
            for w, device in enumerate([across, {"col": partner}]):
                copy = fmcopy(q, 2 * j + w, device)
                copy.start()
                fmcopies.append(copy)
    excopy.wait_recv()
    both = fx[0].astype(F32) + fx[1].astype(F32)
    fx[2] = (extra[...] + first * (both - extra[...])).astype(BF16)
    fxcopy = send_one(fx.at[2], fx.at[3], 2, {"col": other})

    def put(index, src, dst):
        copy = pltpu.make_async_copy(src, dst, out_sem.at[index])
        copy.start()
        return copy

    puts = []
    wait_recv(*row, 0, send4, recv4, s4, r4, 3)
    @pl.loop(0, row_devices)
    def _(c):
        conv = recv4[0, c].astype(F32) + gain[c] * prod[0, c].astype(F32)
        grad_query[c] = (go[c].astype(F32) * conv).astype(BF16)

    puts.append(put(0, grad_query, grad_query_hbm))

    fxcopy.wait_recv()
    extra[...] = fx[3].astype(F32) * side.astype(F32)
    top = lax.broadcasted_iota(jnp.int32, (8, span), 0) == 0
    loads[17].wait()
    for k in reversed(range(col_devices)):
        if (k + 1) % chunk == 0:
            fmcopy((col_devices - 1 - k) // chunk, 0, {"col": partner}).wait_recv()
        tile = jnp.concatenate([fown[k], fmrecv[k]], axis=0)
        tile = jnp.dot(merge[side], tile, preferred_element_type=F32)
        re = jnp.where(top, tile[:8] + extra[2 * k : 2 * k + 1], tile[:8])
        im = jnp.where(top, tile[keep : keep + 8] + extra[2 * k + 1 : 2 * k + 2], tile[keep : keep + 8])
        tile = jnp.concatenate([re, tile[8:keep], im, tile[keep + 8 :]], axis=0)
        flip[pl.ds(k, span, stride=col_devices), : 2 * keep] = tile.T
    for t in range(col_devices):
        lanes = slice(t * span, (t + 1) * span)
        tile = flip[lanes, : 2 * keep].T.astype(BF16)
        filter_grad[:, :, lanes] = tile.reshape(2, keep, span)
    puts.append(put(1, filter_grad, filter_grad_hbm))

    for a in range(2):
        wait_send(*row, a, prod, recv1, s1, r1)
        wait_send(*col, a, send2, recv2, s2, r2)
        wait_send(*col, a, send3, recv3, s3, r3)
    wait_recv(*row, 1, send4, recv4, s4, r4, 3)
    @pl.loop(0, row_devices)
    def _(c):
        mixed_grad = recv4[1, c].astype(F32) + gain[c] * prod[1, c].astype(F32)
        grad_key[c] = (mixed_grad * vi[c].astype(F32)).astype(BF16)
        grad_value[c] = (mixed_grad * gk[c].astype(F32)).astype(BF16)

    puts.append(put(2, grad_key, grad_key_hbm))
    puts.append(put(3, grad_value, grad_value_hbm))

    for a in range(2):
        wait_send(*row, a, send4, recv4, s4, r4)
    for q in range(chunks):
        fcopy(q).wait_send()
    for copy in fmcopies + [mirror, mirror_far, excopy, fxcopy]:
        copy.wait_send()
    for copy in puts:
        copy.wait()


def hand_over(*refs):
    sources, results, held, sems = refs[:4], refs[4:8], refs[8:12], refs[12]
    gets = [pltpu.make_async_copy(sources[i], held[i], sems.at[0, i]) for i in range(4)]
    puts = [pltpu.make_async_copy(held[i], results[i], sems.at[1, i]) for i in range(4)]
    for copy in gets:
        copy.start()
    for get, put in zip(gets, puts):
        get.wait()
        put.start()
    for copy in puts:
        copy.wait()


def shards(tables, row_devices, col_devices, gate_query, gate_key, value_input, grad_output, filter_spec, skip_gain):
    _, channels, rows_here, span = gate_query.shape
    keep = filter_spec.shape[2]
    cols_total = filter_spec.shape[3]
    rows_total = keep * col_devices
    half = rows_total // 2
    act = keep // 2 + 8
    dims = (row_devices, col_devices, keep, span)
    anywhere = pl.BlockSpec(memory_space=pl.ANY)
    token = jax.ShapeDtypeStruct((channels, rows_here, span), BF16)
    names = [
        "forward_high", "forward_low", "inverse_rows", "twist", "place",
        "inner", "lane_high", "lane_low", "lane_inverse", "flip_lanes", "pick",
        "unpick", "merge", "half_twist",
    ]
    dma = pltpu.SemaphoreType.DMA
    tok = (2, row_devices, rows_here, span)
    mid = (2, col_devices, keep, span)
    grad = (col_devices, 2 * act, span)
    freq = jax.ShapeDtypeStruct((2, keep, cols_total), BF16)
    chunks = (4 if col_devices % 4 == 0 else 2,)
    outs = pl.pallas_call(
        functools.partial(kernel, dims),
        out_shape=[token, token, token, freq],
        in_specs=[anywhere] * 5 + [pl.BlockSpec(memory_space=pltpu.SMEM)] + [anywhere] * len(names),
        out_specs=[anywhere] * 4,
        scratch_shapes=[pltpu.VMEM(token.shape, BF16)] * 4
        + [pltpu.VMEM(freq.shape, BF16)]
        + [pltpu.VMEM(tables[name].shape, tables[name].dtype) for name in names]
        + [pltpu.VMEM(token.shape, BF16)] * 3
        + [pltpu.VMEM(freq.shape, BF16)]
        + [
            pltpu.VMEM((cols_total, 128), F32),
            pltpu.VMEM(tok, BF16),
            pltpu.VMEM(tok, BF16),
            pltpu.VMEM(mid, BF16),
            pltpu.VMEM(mid, BF16),
            pltpu.VMEM(mid, BF16),
            pltpu.VMEM(mid, BF16),
            pltpu.VMEM(tok, BF16),
            pltpu.VMEM(tok, BF16),
            pltpu.VMEM(grad, F32),
            pltpu.VMEM((col_devices, act, 2 * span), F32),
            pltpu.VMEM((2, col_devices, act, 2 * span), F32),
            pltpu.VMEM((2, keep // 2, cols_total), BF16),
            pltpu.VMEM((2 * col_devices, span), F32),
            pltpu.VMEM((2, 2 * col_devices, span), BF16),
            pltpu.VMEM((2, col_devices, act, span), F32),
            pltpu.VMEM((2, col_devices, keep // 2, span), F32),
            pltpu.VMEM(mid[1:], BF16),
            pltpu.VMEM(mid[1:], BF16),
            pltpu.VMEM(mid[1:], BF16),
            pltpu.VMEM(mid[1:], BF16),
            pltpu.VMEM(mid[1:], BF16),
            pltpu.VMEM((2 * col_devices, span), F32),
            pltpu.VMEM((4, 2 * col_devices, span), BF16),
            dma((19,)),
            dma((4,)),
            dma((4, 2)),
            dma((2,)), dma((2,)), dma((2,)), dma((2,)), dma((2,)), dma((2,)), dma((2,)), dma((2,)),
            dma(chunks), dma(chunks),
            dma(chunks), dma(chunks),
            dma((4,)), dma((4,)),
        ],
        compiler_params=pltpu.CompilerParams(
            collective_id=0, has_side_effects=True, vmem_limit_bytes=56 * 1024 * 1024
        ),
        name="hyena_backward",
    )(
        gate_query[0], gate_key[0], value_input[0], grad_output[0], filter_spec[:, 0], skip_gain,
        *[jnp.asarray(tables[name]) for name in names],
    )
    outs = pl.pallas_call(
        hand_over,
        out_shape=[jax.ShapeDtypeStruct(out.shape, out.dtype) for out in outs],
        in_specs=[anywhere] * 4,
        out_specs=[anywhere] * 4,
        scratch_shapes=[pltpu.VMEM(out.shape, out.dtype) for out in outs] + [dma((2, 4))],
        name="hand_over",
    )(*outs)
    return (outs[0][None], outs[1][None], outs[2][None], outs[3][:, None])


def solution(mesh):
    row_devices, col_devices = mesh.shape["row"], mesh.shape["col"]
    tokens = P("dp", None, "row", "col")
    freq = P(None, "row", "col", None)

    def run(gate_query, gate_key, value_input, grad_output, filter_spec, skip_gain):
        tables = make_tables(filter_spec.shape[2], filter_spec.shape[3], col_devices)
        return jax.shard_map(
            functools.partial(shards, tables, row_devices, col_devices),
            mesh=mesh,
            in_specs=(tokens, tokens, tokens, tokens, freq, P()),
            out_specs=(tokens, tokens, tokens, freq),
            check_vma=False,
        )(gate_query, gate_key, value_input, grad_output, filter_spec, skip_gain)

    return run
```
